256 devices in a mesh: row: 32 (over y, x, core), col: 8 (over z).
Axes of the slice: x: 4, y: 4, z: 8, core: 2. Of those that a mesh axis runs over, the one named last changes fastest.
Arguments:
- block_values: bfloat16 [32, 8, 128, 128, 128], P('row', 'col'), may hold values from -50 to 50
- block_index: int32 [32, 8, 2, 128], P('row', 'col'), may hold values from 0 to 255, as said below
- block_count: int32 [32, 8], P('row', 'col'), may hold values from 1 to 128
- start_vectors: float32 [32768, 256], P(('row', 'col')), may hold values from -40 to 40
Outputs:
- basis: float32 [32768, 256], P(('row', 'col'))
- projected: float32 [256, 256], replicated
- ritz_residual: float32 [32768, 256], P(('row', 'col'))
- gram_scaled: float32 [256, 256], replicated
The draws below stay inside these ranges and needn't reach their ends.
Inputs may be any that keep to these rules, and one draw needn't show every extreme that they name: Every slot of the device at row index r and col index c holds a pair (i, j) = (block_index[r, c, 0, s], block_index[r, c, 1, s]) with i // 8 = r and j % 8 = c. The slots below block_count[r, c] hold distinct blocks with i <= j; the later slots hold pairs that are not part of the matrix.
All inputs are finite; a program needn't handle non-finite values.
Results may differ from the reference program's by a relative error of at most 0.0051.
Values may be sent and summed in bfloat16 or wider, within the bound.
A program may use at most 128 MiB of HBM per device.

```python
import math
import jax
import jax.numpy as jnp
from jax import lax

BS = 128
K = 256
ITERS = 2
CAP = 128
NROWS = 32768
N_ROW = 32
N_COL = 8


def block_lists(key):
    key_count, key_pick, key_top = jax.random.split(key, 3)
    grid_size = N_ROW * N_COL
    row_pos = jnp.arange(N_ROW, dtype=jnp.int32)[:, None]
    col_pos = jnp.arange(N_COL, dtype=jnp.int32)[None, :]
    eligible = (N_ROW - 1 - row_pos) * N_COL + col_pos + 1
    share = jax.random.randint(key_count, (N_ROW, N_COL), 50, 101, dtype=jnp.int32)
    counts = jnp.maximum(1, eligible * CAP * share // (grid_size * 100))
    top_col = jax.random.randint(key_top, (), 0, N_COL, dtype=jnp.int32)
    counts = jnp.where((row_pos == 0) & (col_pos == top_col), CAP, counts)
    full_shape = (N_ROW, N_COL, N_COL, N_ROW)
    row_dev = jnp.arange(N_ROW, dtype=jnp.int32).reshape(N_ROW, 1, 1, 1)
    col_dev = jnp.arange(N_COL, dtype=jnp.int32).reshape(1, N_COL, 1, 1)
    local_row = jnp.arange(N_COL, dtype=jnp.int32).reshape(1, 1, N_COL, 1)
    local_col = jnp.arange(N_ROW, dtype=jnp.int32).reshape(1, 1, 1, N_ROW)
    first_block = jnp.broadcast_to(row_dev * N_COL + local_row, full_shape)
    second_block = jnp.broadcast_to(local_col * N_COL + col_dev, full_shape)
    place = jnp.broadcast_to(local_row * N_ROW + local_col, full_shape)
    noise = jax.random.randint(key_pick, full_shape, 0, 2 ** 20, dtype=jnp.int32)
    upper_score = (1 + noise) * grid_size + place
    lower_score = 2 ** 21 * grid_size + place
    score = jnp.where(first_block == second_block, 0, jnp.where(first_block < second_block, upper_score, lower_score))
    order = jnp.argsort(score.reshape(N_ROW, N_COL, grid_size), axis=-1, stable=True)[:, :, :CAP]
    first_pick = jnp.take_along_axis(first_block.reshape(N_ROW, N_COL, grid_size), order, axis=-1)
    second_pick = jnp.take_along_axis(second_block.reshape(N_ROW, N_COL, grid_size), order, axis=-1)
    index = jnp.stack([first_pick, second_pick], axis=2)
    return (index.astype(jnp.int32), counts.astype(jnp.int32))


def draw_block_index(key, part):
    index, counts = block_lists(key)
    return index


def draw_block_count(key, part):
    index, counts = block_lists(key)
    return counts


def draw_block_values(key, part):
    key = jax.random.fold_in(key, 11)
    key_base, key_rows, key_cols = jax.random.split(key, 3)
    full_shape = (N_ROW, N_COL, CAP, BS, BS)
    base = jnp.clip(jax.random.normal(key_base, full_shape, jnp.float32), -5.0, 5.0)
    log_range = math.log(10.0)
    row_scale = jnp.exp(log_range * jax.random.uniform(key_rows, (N_ROW, N_COL, CAP, BS, 1), jnp.float32))
    col_scale = jnp.exp(log_range * jax.random.uniform(key_cols, (N_ROW, N_COL, CAP, 1, BS), jnp.float32))
    return (base * row_scale * col_scale * 0.1).astype(jnp.bfloat16)


def draw_start_vectors(key, part):
    key = jax.random.fold_in(key, 23)
    key_base, key_rows = jax.random.split(key, 2)
    full_shape = (NROWS, K)
    base = jnp.clip(jax.random.normal(key_base, full_shape, jnp.float32), -4.0, 4.0)
    log_range = math.log(10.0)
    row_scale = jnp.exp(log_range * jax.random.uniform(key_rows, (NROWS, 1), jnp.float32))
    return (base * row_scale).astype(jnp.float32)


def setup_inputs(seed: int = 0) -> dict:
    seeds = jax.random.split(jax.random.key(seed), 5)
    block_values = draw_block_values(jax.random.fold_in(seeds[4], 71), 0)
    block_index = draw_block_index(jax.random.fold_in(seeds[4], 71), 0)
    block_count = draw_block_count(jax.random.fold_in(seeds[4], 71), 0)
    start_vectors = draw_start_vectors(jax.random.fold_in(seeds[4], 71), 0)
    return {"block_values": block_values, "block_index": block_index, "block_count": block_count, "start_vectors": start_vectors}


slot_group = 16
highest = lax.Precision.HIGHEST

def orthonormal(tall_block):
    gram_sum = jnp.dot(tall_block.T, tall_block, precision=highest)
    factor = jnp.linalg.cholesky(gram_sum)
    return (jax.scipy.linalg.solve_triangular(factor, tall_block.T, lower=True).T, gram_sum)

def reference(block_values, block_index, block_count, start_vectors):
    devices_all = N_ROW * N_COL
    slot_total = block_values.shape[2]
    vec_width = start_vectors.shape[1]
    values = block_values.reshape(devices_all, slot_total, BS, BS)
    firsts = block_index[:, :, 0, :].reshape(devices_all, slot_total).astype(jnp.int32)
    seconds = block_index[:, :, 1, :].reshape(devices_all, slot_total).astype(jnp.int32)
    counts = block_count.reshape(devices_all).astype(jnp.int32)
    slot_ids = jnp.arange(slot_total, dtype=jnp.int32)

    def degree_step(totals, device_item):
        blocks, first_ids, second_ids, live_count = device_item
        live_mask = (slot_ids < live_count).astype(jnp.float32)[:, None]
        magnitude = jnp.abs(blocks)
        across = lax.optimization_barrier(jnp.sum(magnitude, axis=2, dtype=jnp.float32)) * live_mask
        downward = lax.optimization_barrier(jnp.sum(magnitude, axis=1, dtype=jnp.float32)) * live_mask
        totals = totals.at[first_ids].add(across).at[second_ids].add(downward)
        return (totals, None)
    degree, unused = lax.scan(degree_step, jnp.zeros((devices_all, BS), jnp.float32), (values, firsts, seconds, counts))
    inverse_root = 1.0 / jnp.sqrt(degree / BS + 1e-05)

    def apply_operator(vectors):
        weighted = (inverse_root[:, :, None] * vectors.reshape(devices_all, BS, vec_width)).astype(jnp.bfloat16)

        def device_step(totals, device_item):
            blocks, first_ids, second_ids, live_count = device_item

            def group_step(group_index, inner_sum):
                first_slot = group_index * slot_group
                pieces = lax.dynamic_slice_in_dim(blocks, first_slot, slot_group, 0).astype(jnp.float32)
                row_ids = lax.dynamic_slice_in_dim(first_ids, first_slot, slot_group, 0)
                col_ids = lax.dynamic_slice_in_dim(second_ids, first_slot, slot_group, 0)
                live_mask = (first_slot + jnp.arange(slot_group, dtype=jnp.int32) < live_count).astype(jnp.float32)[:, None, None]
                ahead = jnp.einsum('gab,gbk->gak', pieces, weighted[col_ids].astype(jnp.float32), precision=highest) * live_mask
                behind = jnp.einsum('gba,gbk->gak', pieces, weighted[row_ids].astype(jnp.float32), precision=highest) * live_mask
                return inner_sum.at[row_ids].add(ahead).at[col_ids].add(behind)
            group_count = (live_count + slot_group - 1) // slot_group
            return (lax.fori_loop(0, group_count, group_step, totals), None)
        totals, unused_out = lax.scan(device_step, jnp.zeros((devices_all, BS, vec_width), jnp.float32), (values, firsts, seconds, counts))
        return (inverse_root[:, :, None] * totals).reshape(devices_all * BS, vec_width)
    subspace = start_vectors
    last_gram = jnp.zeros((vec_width, vec_width), jnp.float32)
    for iteration in range(ITERS):
        subspace, last_gram = orthonormal(apply_operator(subspace))
    gram_scaled = last_gram / jnp.sqrt(jnp.mean(last_gram * last_gram) + 1e-06)
    mapped = apply_operator(subspace)
    ritz = jnp.dot(subspace.T, mapped, precision=highest)
    spread = jnp.sqrt(jnp.mean(ritz * ritz) + 1e-06)
    total_rows = devices_all * BS
    residual = (mapped - jnp.dot(subspace, ritz, precision=highest)) * (math.sqrt(total_rows / vec_width) / spread)
    return (subspace * math.sqrt(total_rows), ritz / spread, residual, gram_scaled)
```

```python
import functools
import math

import jax
import jax.numpy as jnp
from jax import lax
from jax.experimental import pallas as pl
from jax.experimental.pallas import tpu as pltpu
from jax.sharding import PartitionSpec as P

APPLIES = 3
MESH = pl.DeviceIdType.MESH
highest = lax.Precision.HIGHEST
f32 = jnp.float32
bf16 = jnp.bfloat16
BS = 128


def kernel(side, n_col, width, table, blocks, start, vec_out, gram_out,
           u, wt, wc, colp, corep, rsend, rrecv, rowp, zrecv, yv, ytv,
           dacc, dcore, dxy, dz, gr, ga, gb, gc, gd,
           s_core, r_core, s_xy, r_xy, s_z, r_z, s_fwd, r_fwd):
    chips = side * side
    n_row = 2 * chips
    row = lax.axis_index("row")
    z = lax.axis_index("col")
    core = lax.rem(row, 2)
    chip = row // 2
    y, x = chip // side, lax.rem(chip, side)
    other = 1 - core

    def sibling():
        return (chip * 2 + other, z)

    def xy_to(p):
        return lax.rem(y + p // side, side) * side + lax.rem(x + lax.rem(p, side), side)

    def xy_from(p):
        return lax.rem(y + side - p // side, side) * side + lax.rem(x + side - lax.rem(p, side), side)

    def z_to(p):
        return lax.rem(z + p, n_col)

    def z_from(p):
        return lax.rem(z + n_col - p, n_col)

    def xy_dev(t):
        return (t * 2 + core, z)

    def z_dev(t):
        return (row, t)

    def remote(src, dst, send, recv, dev):
        return pltpu.make_async_remote_copy(
            src_ref=src, dst_ref=dst, send_sem=send, recv_sem=recv,
            device_id=dev, device_id_type=MESH)

    def each(lo, hi, body):
        def step(i, c):
            body(i)
            return c
        lax.fori_loop(lo, hi, step, 0)

    barrier = pltpu.get_barrier_semaphore()
    pl.semaphore_signal(barrier, inc=1, device_id=sibling(), device_id_type=MESH)
    each(1, chips, lambda p: pl.semaphore_signal(
        barrier, inc=1, device_id=xy_dev(xy_to(p)), device_id_type=MESH))
    each(1, n_col, lambda p: pl.semaphore_signal(
        barrier, inc=1, device_id=z_dev(z_to(p)), device_id_type=MESH))

    dacc[...] = jnp.zeros_like(dacc)
    ones = jnp.ones((8, BS), f32)

    def fill_row(lr):
        def fill(pos, total):
            slot = table[lr * n_row + pos]
            live = (slot > 0).astype(f32)
            block = blocks[jnp.maximum(slot - 1, 0)].astype(f32) * live
            u[pl.ds(pl.multiple_of(lr * BS, BS), BS), pl.ds(pl.multiple_of(pos * BS, BS), BS)] = block.astype(bf16)
            size = jnp.abs(block)
            dacc[pos // chips, lax.rem(pos, chips)] += jnp.sum(size.reshape(BS // 8, 8, BS), axis=0)
            return total + size
        total = lax.fori_loop(0, n_row, fill, jnp.zeros((BS, BS), f32))
        rowp[0, lr, 0:8, 0:BS] = lax.dot_general(
            ones, total, (((1,), (1,)), ((), ())), precision=highest, preferred_element_type=f32)
    each(0, n_col, fill_row)

    pl.semaphore_wait(barrier, 1 + (chips - 1) + (n_col - 1))

    D = APPLIES

    def deg_z(p, lr, slot):
        return remote(rowp.at[0, lr, 0:8, 0:BS], dz.at[p], s_z.at[p], r_z.at[D, p], z_dev(slot))
    each(1, n_col, lambda p: deg_z(p, z_to(p), z_to(p)).start())
    deg_core = remote(dacc.at[other], dcore, s_core.at[0], r_core.at[D], sibling())
    deg_core.start()
    deg_core.wait()
    dacc[core] += dcore[...]

    def deg_xy(p):
        t = xy_to(p)
        return remote(dacc.at[core, t], dxy.at[p], s_xy.at[p], r_xy.at[D, p], xy_dev(t))
    each(1, chips, lambda p: deg_xy(p).start())
    dz[0] = rowp[0, z, 0:8, 0:BS]
    dxy[0] = dacc[core, chip]
    each(1, n_col, lambda p: deg_z(p, z_to(p), z_to(p)).wait())
    each(1, chips, lambda p: deg_xy(p).wait())
    degree = jnp.sum(dz[...], axis=0)[0:1] + jnp.sum(jnp.sum(dxy[...], axis=0), axis=0, keepdims=True)
    inv_row = 1.0 / jnp.sqrt(degree / BS + 1e-05)
    inv = jnp.broadcast_to(inv_row, (BS, BS)).T
    inv = inv[:, 0:1]
    yv[0] = start[...]

    def row_pos(k, t):
        return k * chips + t

    def apply_once(a):
        w = inv * yv[a]
        wc[lax.rem(a, 2), pl.ds(pl.multiple_of(row_pos(core, chip) * BS, BS), BS), :] = w.astype(bf16)
        wt[a, :, pl.ds(pl.multiple_of(z * BS, BS), BS)] = w.T.astype(bf16)
        even = lax.rem(a, 2)

        def wt_part(t):
            return wt.at[a, :, pl.ds(pl.multiple_of(t * BS, BS), BS)]

        def wc_part(k, t):
            return wc.at[even, pl.ds(pl.multiple_of(row_pos(k, t) * BS, BS), BS), :]

        def z_send(p):
            return remote(wt_part(z), wt_part(z), s_z.at[p], r_z.at[a, p], z_dev(z_to(p)))

        def z_arrive(p):
            t = z_from(p)
            return remote(wt_part(t), wt_part(t), s_z.at[p], r_z.at[a, p], z_dev(t))

        def xy_send(p):
            return remote(wc_part(core, chip), wc_part(core, chip), s_xy.at[p], r_xy.at[a, p], xy_dev(xy_to(p)))

        def xy_arrive(p):
            t = xy_from(p)
            return remote(wc_part(core, t), wc_part(core, t), s_xy.at[p], r_xy.at[a, p], xy_dev(t))

        def fwd_send(p):
            t = xy_from(p)
            return remote(wc_part(core, t), wc_part(core, t), s_fwd.at[p], r_fwd.at[a, p], sibling())

        def fwd_arrive(p):
            t = xy_from(p)
            return remote(wc_part(other, t), wc_part(other, t), s_fwd.at[p], r_fwd.at[a, p], sibling())

        each(1, n_col, lambda p: z_send(p).start())
        each(1, chips, lambda p: xy_send(p).start())
        fwd_send(0).start()
        each(1, n_col, lambda p: z_arrive(p).wait_recv())

        def col_half(k):
            def tile(n):
                first = (k * chips + 2 * n) * BS
                out = jnp.dot(wt[a], u[:, pl.ds(pl.multiple_of(first, 2 * BS), 2 * BS)], preferred_element_type=f32)
                colp[k, 2 * n] = out[:, :BS]
                colp[k, 2 * n + 1] = out[:, BS:]
            each(0, chips // 2, tile)

        core_swap = remote(colp.at[other], corep.at[a], s_core.at[0], r_core.at[a], sibling())
        col_half(other)
        core_swap.start()
        col_half(core)

        def pass_on(p):
            xy_arrive(p).wait_recv()
            fwd_send(p).start()
        each(1, chips, pass_on)
        core_swap.wait_recv()

        def rs_xy(p):
            return remote(rsend.at[p], rrecv.at[a, p], s_xy.at[p], r_xy.at[APPLIES + 1 + a, p], xy_dev(xy_to(p)))

        def combine(p):
            t = xy_to(p)
            xy_send(p).wait_send()
            rsend[p] = (colp[core, t] + corep[a, t]).astype(bf16)
            rs_xy(p).start()
        each(1, chips, combine)

        each(0, chips, lambda p: fwd_arrive(p).wait_recv())

        def row_tile(n):
            out = jnp.dot(u[pl.ds(pl.multiple_of(n * 2 * BS, 2 * BS), 2 * BS), :], wc[even], preferred_element_type=f32)
            rowp[0, 2 * n] = out[:BS]
            rowp[0, 2 * n + 1] = out[BS:]
        each(0, n_col // 2, row_tile)

        def rs_z(p):
            return remote(rowp.at[0, z_to(p)], zrecv.at[a, p], s_z.at[p], r_z.at[APPLIES + 1 + a, p], z_dev(z_to(p)))

        def row_go(p):
            z_send(p).wait_send()
            rs_z(p).start()
        each(1, n_col, row_go)

        def add_col(p, total):
            rs_xy(p).wait_recv()
            return total + rrecv[a, p].astype(f32)
        cols = lax.fori_loop(1, chips, add_col, colp[core, chip] + corep[a, chip])

        def add_row(p, total):
            rs_z(p).wait_recv()
            return total + zrecv[a, p]
        rows = lax.fori_loop(1, n_col, add_row, rowp[0, z])
        out = inv * (rows + cols.T)
        yv[a + 1] = out
        ytv[a] = out.T
        core_swap.wait_send()
        each(1, chips, lambda p: rs_xy(p).wait_send())
        each(1, n_col, lambda p: rs_z(p).wait_send())
        each(0, chips, lambda p: fwd_send(p).wait_send())

    each(0, APPLIES, apply_once)
    vec_out[0] = yv[2]
    vec_out[1] = yv[3]

    def local_gram(a, b, n):
        g = jnp.dot(ytv[a], yv[b], precision=highest, preferred_element_type=f32)
        g = g.reshape(2, chips, width // n_row, width)
        for k in range(2):
            for t in range(chips):
                gr[k, t, n] = g[k, t]
    local_gram(0, 1, 0)
    local_gram(1, 2, 1)
    local_gram(1, 3, 2)
    A = 2 * APPLIES + 1
    g_core = remote(gr.at[other], ga, s_core.at[0], r_core.at[APPLIES + 1], sibling())
    g_core.start()
    g_core.wait()
    gr[core] += ga[...]

    def g_xy(p):
        t = xy_to(p)
        return remote(gr.at[core, t], gb.at[p], s_xy.at[p], r_xy.at[A, p], xy_dev(t))
    each(1, chips, lambda p: g_xy(p).start())
    each(1, chips, lambda p: g_xy(p).wait())
    gb[0] = gr[core, chip]
    gc[0] = jnp.sum(gb[...], axis=0)

    def g_z(p):
        return remote(gc.at[0], gc.at[p], s_z.at[p], r_z.at[A, p], z_dev(z_to(p)))
    each(1, n_col, lambda p: g_z(p).start())
    each(1, n_col, lambda p: g_z(p).wait())

    def add_z(t, total):
        return total + gc[lax.rem(z + n_col - t, n_col)]
    gd[core, chip] = lax.fori_loop(1, n_col, add_z, gc[z])

    def g_back(p):
        t = xy_from(p)
        return remote(gd.at[core, t], gd.at[core, t], s_xy.at[p], r_xy.at[A + 1, p], xy_dev(t))

    def g_out(p):
        return remote(gd.at[core, chip], gd.at[core, chip], s_xy.at[p], r_xy.at[A + 1, p], xy_dev(xy_to(p)))
    each(1, chips, lambda p: g_out(p).start())
    each(1, chips, lambda p: g_back(p).wait_recv())
    each(1, chips, lambda p: g_out(p).wait_send())
    g_last = remote(gd.at[core], gd.at[core], s_core.at[0], r_core.at[APPLIES + 2], sibling())
    g_last.start()
    g_last.wait_send()
    remote(gd.at[other], gd.at[other], s_core.at[0], r_core.at[APPLIES + 2], sibling()).wait_recv()
    gram_out[...] = gd[...]


def fused(table, blocks, start, side, n_col, interpret=False):
    chips = side * side
    n_row = 2 * chips
    width = start.shape[1]
    sems = pltpu.SemaphoreType.DMA
    vmem = pltpu.VMEM
    part = width // n_row
    return pl.pallas_call(
        functools.partial(kernel, side, n_col, width),
        out_shape=(jax.ShapeDtypeStruct((2, BS, width), f32),
                   jax.ShapeDtypeStruct((2, chips, 3, part, width), f32)),
        in_specs=[pl.BlockSpec(memory_space=pltpu.SMEM)] + [pl.BlockSpec(memory_space=pltpu.VMEM)] * 2,
        out_specs=(pl.BlockSpec(memory_space=pltpu.VMEM), pl.BlockSpec(memory_space=pltpu.VMEM)),
        scratch_shapes=[
            vmem((n_col * BS, n_row * BS), bf16),
            vmem((APPLIES, width, n_col * BS), bf16),
            vmem((2, n_row * BS, width), bf16),
            vmem((2, chips, width, BS), f32),
            vmem((APPLIES, chips, width, BS), f32),
            vmem((chips, width, BS), bf16),
            vmem((APPLIES, chips, width, BS), bf16),
            vmem((1, n_col, BS, width), f32),
            vmem((APPLIES, n_col, BS, width), f32),
            vmem((APPLIES + 1, BS, width), f32),
            vmem((APPLIES, width, BS), f32),
            vmem((2, chips, 8, BS), f32),
            vmem((chips, 8, BS), f32),
            vmem((chips, 8, BS), f32),
            vmem((n_col, 8, BS), f32),
            vmem((2, chips, 3, part, width), f32),
            vmem((chips, 3, part, width), f32),
            vmem((chips, 3, part, width), f32),
            vmem((n_col, 3, part, width), f32),
            vmem((2, chips, 3, part, width), f32),
            sems((1,)), sems((APPLIES + 3,)),
            sems((chips,)), sems((2 * APPLIES + 3, chips)),
            sems((n_col,)), sems((2 * APPLIES + 2, n_col)),
            sems((chips,)), sems((APPLIES, chips)),
        ],
        compiler_params=pltpu.CompilerParams(
            collective_id=0, has_side_effects=True, vmem_limit_bytes=60 * 1024 * 1024),
        interpret=interpret,
    )(table, blocks, start)


def local(block_values, block_index, block_count, start_vectors, interpret=False):
    n_row = lax.axis_size("row")
    n_col = lax.axis_size("col")
    side = math.isqrt(n_row // 2)
    chips = side * side
    blocks = block_values[0, 0]
    slots = blocks.shape[0]
    width = start_vectors.shape[1]
    total_rows = BS * n_row * n_col
    first, second = block_index[0, 0, 0], block_index[0, 0, 1]
    owner = second // n_col
    place = (first % n_col) * n_row + (owner % 2) * chips + owner // 2
    slot_ids = jnp.arange(slots, dtype=jnp.int32)
    place = jnp.where(slot_ids < block_count[0, 0], place, -1)
    spots = jnp.arange(n_row * n_col, dtype=jnp.int32)
    table = jnp.sum(jnp.where(place[None, :] == spots[:, None], slot_ids[None, :] + 1, 0), axis=1)

    vecs, grams = fused(table, blocks, start_vectors, side, n_col, interpret)
    second_vec, third_vec = vecs[0], vecs[1]
    grams = grams.transpose(2, 0, 1, 3, 4).reshape(3, width, width)
    factors = jnp.linalg.cholesky(grams[:2])
    inverses = jax.scipy.linalg.solve_triangular(
        factors, jnp.broadcast_to(jnp.eye(width, dtype=f32), (2, width, width)), lower=True)
    mul = functools.partial(jnp.matmul, precision=highest)
    gram = mul(mul(inverses[0], grams[1]), inverses[0].T)
    ritz = mul(mul(inverses[1], grams[2]), inverses[1].T)
    subspace = mul(second_vec, inverses[1].T)
    mapped = mul(third_vec, inverses[1].T)
    gram_scaled = gram / jnp.sqrt(jnp.mean(gram * gram) + 1e-06)
    spread = jnp.sqrt(jnp.mean(ritz * ritz) + 1e-06)
    residual = (mapped - mul(subspace, ritz)) * (math.sqrt(total_rows / width) / spread)
    return (subspace * math.sqrt(total_rows), ritz / spread, residual, gram_scaled)


def solution(mesh):
    return jax.shard_map(
        local,
        mesh=mesh,
        in_specs=(
            P("row", "col", None, None, None),
            P("row", "col", None, None),
            P("row", "col"),
            P(("row", "col"), None),
        ),
        out_specs=(P(("row", "col"), None), P(), P(("row", "col"), None), P()),
        check_vma=False,
    )
```

```python
import functools
import math

import jax
import jax.numpy as jnp
from jax import lax
from jax.experimental import pallas as pl
from jax.experimental.pallas import tpu as pltpu
from jax.sharding import PartitionSpec as P

APPLIES = 3
MESH = pl.DeviceIdType.MESH
highest = lax.Precision.HIGHEST
f32 = jnp.float32
bf16 = jnp.bfloat16
BS = 128


def kernel(side, n_col, width, table, blocks, start, vec_out, gram_out,
           u, wt, wc, colp, corep, rsend, rrecv, rowp, zrecv, yv, ytv,
           dacc, dcore, dxy, dz, gr, ga, gb, gc, gd,
           s_core, r_core, s_xy, r_xy, s_z, r_z, s_fwd, r_fwd):
    chips = side * side
    n_row = 2 * chips
    row = lax.axis_index("row")
    z = lax.axis_index("col")
    core = lax.rem(row, 2)
    chip = row // 2
    y, x = chip // side, lax.rem(chip, side)
    other = 1 - core

    def sibling():
        return (chip * 2 + other, z)

    def xy_to(p):
        return lax.rem(y + p // side, side) * side + lax.rem(x + lax.rem(p, side), side)

    def xy_from(p):
        return lax.rem(y + side - p // side, side) * side + lax.rem(x + side - lax.rem(p, side), side)

    def z_to(p):
        return lax.rem(z + p, n_col)

    def z_from(p):
        return lax.rem(z + n_col - p, n_col)

    def xy_dev(t):
        return (t * 2 + core, z)

    def z_dev(t):
        return (row, t)

    def remote(src, dst, send, recv, dev):
        return pltpu.make_async_remote_copy(
            src_ref=src, dst_ref=dst, send_sem=send, recv_sem=recv,
            device_id=dev, device_id_type=MESH)

    def each(lo, hi, body):
        def step(i, c):
            body(i)
            return c
        lax.fori_loop(lo, hi, step, 0)

    barrier = pltpu.get_barrier_semaphore()
    pl.semaphore_signal(barrier, inc=1, device_id=sibling(), device_id_type=MESH)
    each(1, chips, lambda p: pl.semaphore_signal(
        barrier, inc=1, device_id=xy_dev(xy_to(p)), device_id_type=MESH))
    each(1, n_col, lambda p: pl.semaphore_signal(
        barrier, inc=1, device_id=z_dev(z_to(p)), device_id_type=MESH))

    dacc[...] = jnp.zeros_like(dacc)
    ones = jnp.ones((8, BS), f32)

    def fill_row(lr):
        def fill(pos, total):
            slot = table[lr * n_row + pos]
            live = (slot > 0).astype(f32)
            block = blocks[jnp.maximum(slot - 1, 0)].astype(f32) * live
            u[pl.ds(pl.multiple_of(lr * BS, BS), BS), pl.ds(pl.multiple_of(pos * BS, BS), BS)] = block.astype(bf16)
            size = jnp.abs(block)
            dacc[pos // chips, lax.rem(pos, chips)] += jnp.sum(size.reshape(BS // 8, 8, BS), axis=0)
            return total + size
        total = lax.fori_loop(0, n_row, fill, jnp.zeros((BS, BS), f32))
        rowp[0, lr, 0:8, 0:BS] = lax.dot_general(
            ones, total, (((1,), (1,)), ((), ())), precision=highest, preferred_element_type=f32)
    each(0, n_col, fill_row)

    pl.semaphore_wait(barrier, 1 + (chips - 1) + (n_col - 1))

    D = APPLIES

    def deg_z(p, lr, slot):
        return remote(rowp.at[0, lr, 0:8, 0:BS], dz.at[p], s_z.at[p], r_z.at[D, p], z_dev(slot))
    each(1, n_col, lambda p: deg_z(p, z_to(p), z_to(p)).start())
    deg_core = remote(dacc.at[other], dcore, s_core.at[0], r_core.at[D], sibling())
    deg_core.start()
    deg_core.wait()
    dacc[core] += dcore[...]

    def deg_xy(p):
        t = xy_to(p)
        return remote(dacc.at[core, t], dxy.at[p], s_xy.at[p], r_xy.at[D, p], xy_dev(t))
    each(1, chips, lambda p: deg_xy(p).start())
    dz[0] = rowp[0, z, 0:8, 0:BS]
    dxy[0] = dacc[core, chip]
    each(1, n_col, lambda p: deg_z(p, z_to(p), z_to(p)).wait())
    each(1, chips, lambda p: deg_xy(p).wait())
    degree = jnp.sum(dz[...], axis=0)[0:1] + jnp.sum(jnp.sum(dxy[...], axis=0), axis=0, keepdims=True)
    inv_row = 1.0 / jnp.sqrt(degree / BS + 1e-05)
    inv = jnp.broadcast_to(inv_row, (BS, BS)).T
    inv = inv[:, 0:1]
    yv[0] = start[...]

    def row_pos(k, t):
        return k * chips + t

    def apply_once(a):
        w = inv * yv[a]
        wc[lax.rem(a, 2), pl.ds(pl.multiple_of(row_pos(core, chip) * BS, BS), BS), :] = w.astype(bf16)
        wt[a, :, pl.ds(pl.multiple_of(z * BS, BS), BS)] = w.T.astype(bf16)
        even = lax.rem(a, 2)

        def wt_part(t):
            return wt.at[a, :, pl.ds(pl.multiple_of(t * BS, BS), BS)]

        def wc_part(k, t):
            return wc.at[even, pl.ds(pl.multiple_of(row_pos(k, t) * BS, BS), BS), :]

        def z_send(p):
            return remote(wt_part(z), wt_part(z), s_z.at[p], r_z.at[a, p], z_dev(z_to(p)))

        def z_arrive(p):
            t = z_from(p)
            return remote(wt_part(t), wt_part(t), s_z.at[p], r_z.at[a, p], z_dev(t))

        def xy_send(p):
            return remote(wc_part(core, chip), wc_part(core, chip), s_xy.at[p], r_xy.at[a, p], xy_dev(xy_to(p)))

        def xy_arrive(p):
            t = xy_from(p)
            return remote(wc_part(core, t), wc_part(core, t), s_xy.at[p], r_xy.at[a, p], xy_dev(t))

        def fwd_send(p):
            t = xy_from(p)
            return remote(wc_part(core, t), wc_part(core, t), s_fwd.at[p], r_fwd.at[a, p], sibling())

        def fwd_arrive(p):
            t = xy_from(p)
            return remote(wc_part(other, t), wc_part(other, t), s_fwd.at[p], r_fwd.at[a, p], sibling())

        each(1, n_col, lambda p: z_send(p).start())
        each(1, chips, lambda p: xy_send(p).start())
        fwd_send(0).start()
        each(1, n_col, lambda p: z_arrive(p).wait_recv())

        def col_half(k):
            def tile(n):
                first = (k * chips + 2 * n) * BS
                out = jnp.dot(wt[a], u[:, pl.ds(pl.multiple_of(first, 2 * BS), 2 * BS)], preferred_element_type=f32)
                colp[k, 2 * n] = out[:, :BS]
                colp[k, 2 * n + 1] = out[:, BS:]
            each(0, chips // 2, tile)

        core_swap = remote(colp.at[other], corep.at[a], s_core.at[0], r_core.at[a], sibling())
        col_half(other)
        core_swap.start()
        col_half(core)

        def pass_on(p):
            xy_arrive(p).wait_recv()
            fwd_send(p).start()
        each(1, chips, pass_on)
        core_swap.wait_recv()

        def rs_xy(p):
            return remote(rsend.at[p], rrecv.at[a, p], s_xy.at[p], r_xy.at[APPLIES + 1 + a, p], xy_dev(xy_to(p)))

        def combine(p):
            t = xy_to(p)
            xy_send(p).wait_send()
            rsend[p] = (colp[core, t] + corep[a, t]).astype(bf16)
            rs_xy(p).start()
        each(1, chips, combine)

        each(0, chips, lambda p: fwd_arrive(p).wait_recv())

        def row_tile(n):
            out = jnp.dot(u[pl.ds(pl.multiple_of(n * 2 * BS, 2 * BS), 2 * BS), :], wc[even], preferred_element_type=f32)
            rowp[0, 2 * n] = out[:BS]
            rowp[0, 2 * n + 1] = out[BS:]
        each(0, n_col // 2, row_tile)

        def rs_z(p):
            return remote(rowp.at[0, z_to(p)], zrecv.at[a, p], s_z.at[p], r_z.at[APPLIES + 1 + a, p], z_dev(z_to(p)))

        def row_go(p):
            z_send(p).wait_send()
            rs_z(p).start()
        each(1, n_col, row_go)

        def add_col(p, total):
            rs_xy(p).wait_recv()
            return total + rrecv[a, p].astype(f32)
        cols = lax.fori_loop(1, chips, add_col, colp[core, chip] + corep[a, chip])

        def add_row(p, total):
            rs_z(p).wait_recv()
            return total + zrecv[a, p]
        rows = lax.fori_loop(1, n_col, add_row, rowp[0, z])
        out = inv * (rows + cols.T)
        yv[a + 1] = out
        ytv[a] = out.T
        core_swap.wait_send()
        each(1, chips, lambda p: rs_xy(p).wait_send())
        each(1, n_col, lambda p: rs_z(p).wait_send())
        each(0, chips, lambda p: fwd_send(p).wait_send())

    each(0, APPLIES, apply_once)
    vec_out[0] = yv[2]
    vec_out[1] = yv[3]

    def local_gram(a, b, n):
        g = jnp.dot(ytv[a], yv[b], precision=highest, preferred_element_type=f32)
        g = g.reshape(2, chips, width // n_row, width)
        for k in range(2):
            for t in range(chips):
                gr[k, t, n] = g[k, t]
    local_gram(0, 1, 0)
    local_gram(1, 2, 1)
    local_gram(1, 3, 2)
    A = 2 * APPLIES + 1
    g_core = remote(gr.at[other], ga, s_core.at[0], r_core.at[APPLIES + 1], sibling())
    g_core.start()
    g_core.wait()
    gr[core] += ga[...]

    def g_xy(p):
        t = xy_to(p)
        return remote(gr.at[core, t], gb.at[p], s_xy.at[p], r_xy.at[A, p], xy_dev(t))
    each(1, chips, lambda p: g_xy(p).start())
    each(1, chips, lambda p: g_xy(p).wait())
    gb[0] = gr[core, chip]
    gc[0] = jnp.sum(gb[...], axis=0)

    def g_z(p):
        return remote(gc.at[0], gc.at[p], s_z.at[p], r_z.at[A, p], z_dev(z_to(p)))
    each(1, n_col, lambda p: g_z(p).start())
    each(1, n_col, lambda p: g_z(p).wait())

    def add_z(t, total):
        return total + gc[lax.rem(z + n_col - t, n_col)]
    gd[core, chip] = lax.fori_loop(1, n_col, add_z, gc[z])

    def g_back(p):
        t = xy_from(p)
        return remote(gd.at[core, t], gd.at[core, t], s_xy.at[p], r_xy.at[A + 1, p], xy_dev(t))

    def g_out(p):
        return remote(gd.at[core, chip], gd.at[core, chip], s_xy.at[p], r_xy.at[A + 1, p], xy_dev(xy_to(p)))
    each(1, chips, lambda p: g_out(p).start())
    each(1, chips, lambda p: g_back(p).wait_recv())
    each(1, chips, lambda p: g_out(p).wait_send())
    g_last = remote(gd.at[core], gd.at[core], s_core.at[0], r_core.at[APPLIES + 2], sibling())
    g_last.start()
    g_last.wait_send()
    remote(gd.at[other], gd.at[other], s_core.at[0], r_core.at[APPLIES + 2], sibling()).wait_recv()
    gram_out[...] = gd[...]


def fused(table, blocks, start, side, n_col, interpret=False):
    chips = side * side
    n_row = 2 * chips
    width = start.shape[1]
    sems = pltpu.SemaphoreType.DMA
    vmem = pltpu.VMEM
    part = width // n_row
    return pl.pallas_call(
        functools.partial(kernel, side, n_col, width),
        out_shape=(jax.ShapeDtypeStruct((2, BS, width), f32),
                   jax.ShapeDtypeStruct((2, chips, 3, part, width), f32)),
        in_specs=[pl.BlockSpec(memory_space=pltpu.SMEM)] + [pl.BlockSpec(memory_space=pltpu.VMEM)] * 2,
        out_specs=(pl.BlockSpec(memory_space=pltpu.VMEM), pl.BlockSpec(memory_space=pltpu.VMEM)),
        scratch_shapes=[
            vmem((n_col * BS, n_row * BS), bf16),
            vmem((APPLIES, width, n_col * BS), bf16),
            vmem((2, n_row * BS, width), bf16),
            vmem((2, chips, width, BS), f32),
            vmem((APPLIES, chips, width, BS), f32),
            vmem((chips, width, BS), bf16),
            vmem((APPLIES, chips, width, BS), bf16),
            vmem((1, n_col, BS, width), f32),
            vmem((APPLIES, n_col, BS, width), f32),
            vmem((APPLIES + 1, BS, width), f32),
            vmem((APPLIES, width, BS), f32),
            vmem((2, chips, 8, BS), f32),
            vmem((chips, 8, BS), f32),
            vmem((chips, 8, BS), f32),
            vmem((n_col, 8, BS), f32),
            vmem((2, chips, 3, part, width), f32),
            vmem((chips, 3, part, width), f32),
            vmem((chips, 3, part, width), f32),
            vmem((n_col, 3, part, width), f32),
            vmem((2, chips, 3, part, width), f32),
            sems((1,)), sems((APPLIES + 3,)),
            sems((chips,)), sems((2 * APPLIES + 3, chips)),
            sems((n_col,)), sems((2 * APPLIES + 2, n_col)),
            sems((chips,)), sems((APPLIES, chips)),
        ],
        compiler_params=pltpu.CompilerParams(
            collective_id=0, has_side_effects=True, vmem_limit_bytes=60 * 1024 * 1024),
        interpret=interpret,
    )(table, blocks, start)


def tri_inverses(n, s, e):
    sub = lax.broadcasted_iota(jnp.int32, (8, BS), 0)
    lane = lax.broadcasted_iota(jnp.int32, (8, BS), 1)
    eye = (lax.broadcasted_iota(jnp.int32, (BS, BS), 0) == lax.broadcasted_iota(jnp.int32, (BS, BS), 1)).astype(f32)
    for m in range(n):
        e[m] = eye

    def panel(k, c):
        first = pl.multiple_of(k * 8, 8)
        for m in range(n):
            r = s[m, pl.ds(first, 8), :]
            g = e[m, pl.ds(first, 8), :]
            own = jnp.where(lane >= first, jnp.where(lane < first + 8, r, 0.0), 0.0)
            cols = []
            for j in range(8):
                at_j = jnp.where(lane == first + j, own, 0.0)
                cols.append(jnp.broadcast_to(jnp.sum(at_j, axis=1, keepdims=True), (8, BS)))
            scale = jnp.zeros((8, BS), f32)
            for j in range(8):
                pivot = jnp.broadcast_to(cols[j][j:j + 1], (8, BS))
                mult = jnp.where(sub > j, cols[j] / pivot, 0.0)
                scale = jnp.where(sub == j, pivot, scale)
                r = r - mult * r[j:j + 1]
                g = g - mult * g[j:j + 1]
                for i in range(j + 1, 8):
                    cols[i] = cols[i] - mult * cols[i][j:j + 1]
            scale = 1.0 / jnp.sqrt(scale)
            v = r * scale
            g = g * scale
            e[m, pl.ds(first, 8), :] = g
            below = jnp.where(lane >= first + 8, v, 0.0)
            step = lax.dot_general(below, jnp.concatenate([v, g], axis=1), (((0,), (0,)), ((), ())),
                                   precision=highest, preferred_element_type=f32)
            s[m] -= step[:, :BS]
            e[m] -= step[:, BS:]
        return c
    lax.fori_loop(0, BS // 8, panel, 0)


def finish_kernel(total_rows, vecs, grams, basis, projected, residual, scaled, s, e, li):
    width = vecs.shape[2]
    mul = functools.partial(jnp.dot, precision=highest, preferred_element_type=f32)
    g = [grams[:, :, m].reshape(width, width) for m in range(3)]
    half = []
    for m in range(2):
        s[m] = g[m][:BS, :BS]
    tri_inverses(2, s, e)
    for m in range(2):
        li[m, :BS, :BS] = e[m]
        li[m, :BS, BS:] = jnp.zeros((BS, BS), f32)
        half.append(mul(e[m], g[m][:BS, BS:]))
        s[m] = g[m][BS:, BS:] - lax.dot_general(
            half[m], half[m], (((0,), (0,)), ((), ())), precision=highest, preferred_element_type=f32)
    tri_inverses(2, s, e)
    for m in range(2):
        li[m, BS:, BS:] = e[m]
        cross = lax.dot_general(half[m], li[m, :BS, :BS], (((0,), (0,)), ((), ())),
                                precision=highest, preferred_element_type=f32)
        li[m, BS:, :BS] = -mul(e[m], cross)
    gram = mul(mul(li[0], g[1]), li[0].T)
    right = li[1].T
    ritz = mul(mul(li[1], g[2]), right)
    subspace = mul(vecs[0], right)
    mapped = mul(vecs[1], right)
    area = width * width
    scaled[...] = gram / jnp.sqrt(jnp.sum(gram * gram, keepdims=True) / area + 1e-06)
    spread = jnp.sqrt(jnp.sum(ritz * ritz, keepdims=True) / area + 1e-06)
    projected[...] = ritz / spread
    basis[...] = subspace * math.sqrt(total_rows)
    residual[...] = (mapped - mul(subspace, ritz)) * (math.sqrt(total_rows / width) / spread)


def finish(vecs, grams, total_rows, interpret=False):
    width = vecs.shape[2]
    tall = jax.ShapeDtypeStruct((BS, width), f32)
    square = jax.ShapeDtypeStruct((width, width), f32)
    return pl.pallas_call(
        functools.partial(finish_kernel, total_rows),
        out_shape=(tall, square, tall, square),
        in_specs=[pl.BlockSpec(memory_space=pltpu.VMEM)] * 2,
        out_specs=tuple([pl.BlockSpec(memory_space=pltpu.VMEM)] * 4),
        scratch_shapes=[pltpu.VMEM((2, BS, BS), f32), pltpu.VMEM((2, BS, BS), f32),
                        pltpu.VMEM((2, width, width), f32)],
        compiler_params=pltpu.CompilerParams(vmem_limit_bytes=32 * 1024 * 1024),
        interpret=interpret,
    )(vecs, grams)


def local(block_values, block_index, block_count, start_vectors, interpret=False):
    n_row = lax.axis_size("row")
    n_col = lax.axis_size("col")
    side = math.isqrt(n_row // 2)
    chips = side * side
    blocks = block_values[0, 0]
    slots = blocks.shape[0]
    width = start_vectors.shape[1]
    total_rows = BS * n_row * n_col
    first, second = block_index[0, 0, 0], block_index[0, 0, 1]
    owner = second // n_col
    place = (first % n_col) * n_row + (owner % 2) * chips + owner // 2
    slot_ids = jnp.arange(slots, dtype=jnp.int32)
    place = jnp.where(slot_ids < block_count[0, 0], place, -1)
    spots = jnp.arange(n_row * n_col, dtype=jnp.int32)
    table = jnp.sum(jnp.where(place[None, :] == spots[:, None], slot_ids[None, :] + 1, 0), axis=1)

    vecs, grams = fused(table, blocks, start_vectors, side, n_col, interpret)
    return finish(vecs, grams, total_rows, interpret)


def solution(mesh):
    return jax.shard_map(
        local,
        mesh=mesh,
        in_specs=(
            P("row", "col", None, None, None),
            P("row", "col", None, None),
            P("row", "col"),
            P(("row", "col"), None),
        ),
        out_specs=(P(("row", "col"), None), P(), P(("row", "col"), None), P()),
        check_vma=False,
    )
```

```python
import functools
import math

import jax
import jax.numpy as jnp
from jax import lax
from jax.experimental import pallas as pl
from jax.experimental.pallas import tpu as pltpu
from jax.sharding import PartitionSpec as P

APPLIES = 3
MESH = pl.DeviceIdType.MESH
highest = lax.Precision.HIGHEST
f32 = jnp.float32
bf16 = jnp.bfloat16
BS = 128


def kernel(side, n_col, width, table, blocks, start, basis, projected, residual, scaled,
           u, wt, wc, colp, colq, corep, rsend, rrecv, rowp, zsend, zrecv, yv, ytv,
           dacc, dcore, dxy, dz, gram_bufs, ritz_bufs, chol,
           s_core, r_core, s_xy, r_xy, s_z, r_z, s_fwd, r_fwd,
           t_core, q_core, t_xy, q_xy, t_z, q_z):
    chips = side * side
    n_row = 2 * chips
    row = lax.axis_index("row")
    z = lax.axis_index("col")
    core = lax.rem(row, 2)
    chip = row // 2
    y, x = chip // side, lax.rem(chip, side)
    other = 1 - core

    def sibling():
        return (chip * 2 + other, z)

    def xy_to(p):
        return lax.rem(y + p // side, side) * side + lax.rem(x + lax.rem(p, side), side)

    def xy_from(p):
        return lax.rem(y + side - p // side, side) * side + lax.rem(x + side - lax.rem(p, side), side)

    def z_to(p):
        return lax.rem(z + p, n_col)

    def z_from(p):
        return lax.rem(z + n_col - p, n_col)

    def xy_dev(t):
        return (t * 2 + core, z)

    def z_dev(t):
        return (row, t)

    def remote(src, dst, send, recv, dev):
        return pltpu.make_async_remote_copy(
            src_ref=src, dst_ref=dst, send_sem=send, recv_sem=recv,
            device_id=dev, device_id_type=MESH)

    def each(lo, hi, body):
        def step(i, c):
            body(i)
            return c
        lax.fori_loop(lo, hi, step, 0)

    barrier = pltpu.get_barrier_semaphore()
    pl.semaphore_signal(barrier, inc=1, device_id=sibling(), device_id_type=MESH)
    each(1, chips, lambda p: pl.semaphore_signal(
        barrier, inc=1, device_id=xy_dev(xy_to(p)), device_id_type=MESH))
    each(1, n_col, lambda p: pl.semaphore_signal(
        barrier, inc=1, device_id=z_dev(z_to(p)), device_id_type=MESH))

    dacc[...] = jnp.zeros_like(dacc)
    ones = jnp.ones((8, BS), f32)

    def fill_row(lr):
        def fill(pos, total):
            slot = table[lr * n_row + pos]
            live = (slot > 0).astype(f32)
            block = blocks[jnp.maximum(slot - 1, 0)].astype(f32) * live
            u[pl.ds(pl.multiple_of(lr * BS, BS), BS), pl.ds(pl.multiple_of(pos * BS, BS), BS)] = block.astype(bf16)
            size = jnp.abs(block)
            dacc[pos // chips, lax.rem(pos, chips)] += jnp.sum(size.reshape(BS // 8, 8, BS), axis=0)
            return total + size
        total = lax.fori_loop(0, n_row, fill, jnp.zeros((BS, BS), f32))
        rowp[0, lr, 0:8, 0:BS] = lax.dot_general(
            ones, total, (((1,), (1,)), ((), ())), precision=highest, preferred_element_type=f32)
    each(0, n_col, fill_row)

    pl.semaphore_wait(barrier, 1 + (chips - 1) + (n_col - 1))

    D = APPLIES

    def deg_z(p, lr, slot):
        return remote(rowp.at[0, lr, 0:8, 0:BS], dz.at[p], s_z.at[p], r_z.at[D, p], z_dev(slot))
    each(1, n_col, lambda p: deg_z(p, z_to(p), z_to(p)).start())
    deg_core = remote(dacc.at[other], dcore, s_core.at[0], r_core.at[D], sibling())
    deg_core.start()
    deg_core.wait()
    dacc[core] += dcore[...]

    def deg_xy(p):
        t = xy_to(p)
        return remote(dacc.at[core, t], dxy.at[p], s_xy.at[p], r_xy.at[D, p], xy_dev(t))
    each(1, chips, lambda p: deg_xy(p).start())
    dz[0] = rowp[0, z, 0:8, 0:BS]
    dxy[0] = dacc[core, chip]
    each(1, n_col, lambda p: deg_z(p, z_to(p), z_to(p)).wait())
    each(1, chips, lambda p: deg_xy(p).wait())
    degree = jnp.sum(dz[...], axis=0)[0:1] + jnp.sum(jnp.sum(dxy[...], axis=0), axis=0, keepdims=True)
    inv_row = 1.0 / jnp.sqrt(degree / BS + 1e-05)
    inv = jnp.broadcast_to(inv_row, (BS, BS)).T
    inv = inv[:, 0:1]
    yv[0] = start[...]

    def row_pos(k, t):
        return k * chips + t

    def apply_once(a, idle_gather=None, idle_scatter=None):
        w = inv * yv[a]
        wc[(a % 2), pl.ds(pl.multiple_of(row_pos(core, chip) * BS, BS), BS), :] = w.astype(bf16)
        wt[a, :, pl.ds(pl.multiple_of(z * BS, BS), BS)] = w.T.astype(bf16)
        even = (a % 2)

        def wt_part(t):
            return wt.at[a, :, pl.ds(pl.multiple_of(t * BS, BS), BS)]

        def wc_part(k, t):
            return wc.at[even, pl.ds(pl.multiple_of(row_pos(k, t) * BS, BS), BS), :]

        def z_send(p):
            return remote(wt_part(z), wt_part(z), s_z.at[p], r_z.at[a, p], z_dev(z_to(p)))

        def z_arrive(p):
            t = z_from(p)
            return remote(wt_part(t), wt_part(t), s_z.at[p], r_z.at[a, p], z_dev(t))

        def xy_send(p):
            return remote(wc_part(core, chip), wc_part(core, chip), s_xy.at[p], r_xy.at[a, p], xy_dev(xy_to(p)))

        def xy_arrive(p):
            t = xy_from(p)
            return remote(wc_part(core, t), wc_part(core, t), s_xy.at[p], r_xy.at[a, p], xy_dev(t))

        def fwd_send(p):
            t = xy_from(p)
            return remote(wc_part(core, t), wc_part(core, t), s_fwd.at[p], r_fwd.at[a, p], sibling())

        def fwd_arrive(p):
            t = xy_from(p)
            return remote(wc_part(other, t), wc_part(other, t), s_fwd.at[p], r_fwd.at[a, p], sibling())

        each(1, n_col, lambda p: z_send(p).start())
        each(1, chips, lambda p: xy_send(p).start())
        fwd_send(0).start()
        if idle_gather is not None:
            idle_gather()
        each(1, n_col, lambda p: z_arrive(p).wait_recv())

        def col_half(k, out_ref):
            def tile(n):
                first = (k * chips + 2 * n) * BS
                out = jnp.dot(wt[a], u[:, pl.ds(pl.multiple_of(first, 2 * BS), 2 * BS)], preferred_element_type=f32)
                out_ref[2 * n] = out[:, :BS].astype(out_ref.dtype)
                out_ref[2 * n + 1] = out[:, BS:].astype(out_ref.dtype)
            each(0, chips // 2, tile)

        core_swap = remote(colq, corep.at[a], s_core.at[0], r_core.at[a], sibling())
        col_half(other, colq)
        core_swap.start()
        col_half(core, colp)

        def pass_on(p):
            xy_arrive(p).wait_recv()
            fwd_send(p).start()
        each(1, chips, pass_on)
        core_swap.wait_recv()

        def rs_xy(p):
            return remote(rsend.at[p], rrecv.at[a, p], s_xy.at[p], r_xy.at[APPLIES + 1 + a, p], xy_dev(xy_to(p)))

        def combine(p):
            t = xy_to(p)
            xy_send(p).wait_send()
            rsend[p] = (colp[t] + corep[a, t].astype(f32)).astype(bf16)
            rs_xy(p).start()
        each(1, chips, combine)

        each(0, chips, lambda p: fwd_arrive(p).wait_recv())

        def row_tile(n):
            out = jnp.dot(u[pl.ds(pl.multiple_of(n * 2 * BS, 2 * BS), 2 * BS), :], wc[even], preferred_element_type=f32)
            rowp[0, 2 * n] = out[:BS]
            rowp[0, 2 * n + 1] = out[BS:]
        each(0, n_col // 2, row_tile)

        def rs_z(p):
            return remote(zsend.at[p], zrecv.at[a, p], s_z.at[p], r_z.at[APPLIES + 1 + a, p], z_dev(z_to(p)))

        def row_go(p):
            z_send(p).wait_send()
            zsend[p] = rowp[0, z_to(p)].astype(bf16)
            rs_z(p).start()
        each(1, n_col, row_go)
        if idle_scatter is not None:
            idle_scatter()

        def add_col(p, total):
            rs_xy(p).wait_recv()
            return total + rrecv[a, p].astype(f32)
        cols = lax.fori_loop(1, chips, add_col, colp[chip] + corep[a, chip].astype(f32))

        def add_row(p, total):
            rs_z(p).wait_recv()
            return total + zrecv[a, p].astype(f32)
        rows = lax.fori_loop(1, n_col, add_row, rowp[0, z])
        out = inv * (rows + cols.T)
        yv[a + 1] = out
        ytv[a] = out.T
        core_swap.wait_send()
        each(1, chips, lambda p: rs_xy(p).wait_send())
        each(1, n_col, lambda p: rs_z(p).wait_send())
        each(0, chips, lambda p: fwd_send(p).wait_send())

    def local_gram(a, b, into, n):
        g = jnp.dot(ytv[a], yv[b], precision=highest, preferred_element_type=f32)
        g = g.reshape(2, chips, width // n_row, width)
        for k in range(2):
            for t in range(chips):
                into[k, t, n] = g[k, t]

    def sum_all(bufs, base, idle):
        gr, ga, gb, gc, gd = bufs
        q = 2 * base
        g_core = remote(gr.at[other], ga, t_core.at[0], q_core.at[q], sibling())
        g_core.start()
        idle(0)
        g_core.wait()
        gr[core] += ga[...]

        def g_xy(p):
            t = xy_to(p)
            return remote(gr.at[core, t], gb.at[p], t_xy.at[p], q_xy.at[q, p], xy_dev(t))
        each(1, chips, lambda p: g_xy(p).start())
        idle(1)
        each(1, chips, lambda p: g_xy(p).wait())
        gb[0] = gr[core, chip]
        gc[0] = jnp.sum(gb[...], axis=0)

        def g_z(p):
            return remote(gc.at[0], gc.at[p], t_z.at[p], q_z.at[base, p], z_dev(z_to(p)))
        each(1, n_col, lambda p: g_z(p).start())
        idle(2)
        each(1, n_col, lambda p: g_z(p).wait())

        def add_z(t, total):
            return total + gc[lax.rem(z + n_col - t, n_col)]
        gd[core, chip] = lax.fori_loop(1, n_col, add_z, gc[z])

        def g_back(p):
            t = xy_from(p)
            return remote(gd.at[core, t], gd.at[core, t], t_xy.at[p], q_xy.at[q + 1, p], xy_dev(t))

        def g_out(p):
            return remote(gd.at[core, chip], gd.at[core, chip], t_xy.at[p], q_xy.at[q + 1, p], xy_dev(xy_to(p)))
        each(1, chips, lambda p: g_out(p).start())
        idle(3)
        each(1, chips, lambda p: g_back(p).wait_recv())
        each(1, chips, lambda p: g_out(p).wait_send())
        g_last = remote(gd.at[core], gd.at[core], t_core.at[0], q_core.at[q + 1], sibling())
        g_last.start()
        idle(4)
        g_last.wait_send()
        remote(gd.at[other], gd.at[other], t_core.at[0], q_core.at[q + 1], sibling()).wait_recv()

    mul = functools.partial(jnp.dot, precision=highest, preferred_element_type=f32)
    tmul = lambda a, b: lax.dot_general(a, b, (((0,), (0,)), ((), ())), precision=highest, preferred_element_type=f32)
    s, e, li, half, full = chol

    def sum_grams():
        local_gram(0, 1, gram_bufs[0], 0)
        local_gram(1, 2, gram_bufs[0], 1)
        sum_all(gram_bufs, 0, lambda i: None)

    def first_factors():
        for m in range(2):
            full[m] = gram_bufs[4][:, :, m].reshape(width, width)
            s[m] = full[m, :BS, :BS]
        unit(e)
        panels(s, e, 0, BS // 8)
        for m in range(2):
            li[m, :BS, :BS] = e[m]
            li[m, :BS, BS:] = jnp.zeros((BS, BS), f32)
            half[m] = mul(e[m], full[m, :BS, BS:])
            s[m] = full[m, BS:, BS:] - tmul(half[m], half[m])
        unit(e)

    each(0, APPLIES - 1, apply_once)
    apply_once(APPLIES - 1, sum_grams, first_factors)
    local_gram(1, 3, ritz_bufs[0], 0)
    cuts = (0, 2, 7, 11, 16)

    def second_factors(i):
        if i < 4:
            panels(s, e, cuts[i], cuts[i + 1])
        else:
            for m in range(2):
                li[m, BS:, BS:] = e[m]
                li[m, BS:, :BS] = -mul(e[m], tmul(half[m], li[m, :BS, :BS]))
            gram = mul(mul(li[0], full[1]), li[0].T)
            scaled[...] = gram / jnp.sqrt(jnp.sum(gram * gram, keepdims=True) / (width * width) + 1e-06)
            full[0] = li[1].T
            yv[0] = mul(yv[2], full[0])
            yv[1] = mul(yv[3], full[0])

    sum_all(ritz_bufs, 1, second_factors)
    total_rows = BS * n_row * n_col
    ritz = mul(mul(li[1], ritz_bufs[4][:, :, 0].reshape(width, width)), full[0])
    spread = jnp.sqrt(jnp.sum(ritz * ritz, keepdims=True) / (width * width) + 1e-06)
    projected[...] = ritz / spread
    basis[...] = yv[0] * math.sqrt(total_rows)
    residual[...] = (yv[1] - mul(yv[0], ritz)) * (math.sqrt(total_rows / width) / spread)


def unit(e):
    eye = (lax.broadcasted_iota(jnp.int32, (BS, BS), 0) == lax.broadcasted_iota(jnp.int32, (BS, BS), 1)).astype(f32)
    for m in range(2):
        e[m] = eye


def fused(table, blocks, start, side, n_col, interpret=False):
    chips = side * side
    n_row = 2 * chips
    width = start.shape[1]
    sems = pltpu.SemaphoreType.DMA
    vmem = pltpu.VMEM
    part = width // n_row
    tall = jax.ShapeDtypeStruct((BS, width), f32)
    square = jax.ShapeDtypeStruct((width, width), f32)

    def sum_bufs(n):
        return (vmem((2, chips, n, part, width), f32), vmem((chips, n, part, width), f32),
                vmem((chips, n, part, width), f32), vmem((n_col, n, part, width), f32),
                vmem((2, chips, n, part, width), f32))
    return pl.pallas_call(
        functools.partial(kernel, side, n_col, width),
        out_shape=(tall, square, tall, square),
        in_specs=[pl.BlockSpec(memory_space=pltpu.SMEM)] + [pl.BlockSpec(memory_space=pltpu.VMEM)] * 2,
        out_specs=tuple([pl.BlockSpec(memory_space=pltpu.VMEM)] * 4),
        scratch_shapes=[
            vmem((n_col * BS, n_row * BS), bf16),
            vmem((APPLIES, width, n_col * BS), bf16),
            vmem((2, n_row * BS, width), bf16),
            vmem((chips, width, BS), f32),
            vmem((chips, width, BS), bf16),
            vmem((APPLIES, chips, width, BS), bf16),
            vmem((chips, width, BS), bf16),
            vmem((APPLIES, chips, width, BS), bf16),
            vmem((1, n_col, BS, width), f32),
            vmem((n_col, BS, width), bf16),
            vmem((APPLIES, n_col, BS, width), bf16),
            vmem((APPLIES + 1, BS, width), f32),
            vmem((APPLIES, width, BS), f32),
            vmem((2, chips, 8, BS), f32),
            vmem((chips, 8, BS), f32),
            vmem((chips, 8, BS), f32),
            vmem((n_col, 8, BS), f32),
            sum_bufs(2), sum_bufs(1),
            (vmem((2, BS, BS), f32), vmem((2, BS, BS), f32), vmem((2, width, width), f32),
             vmem((2, BS, BS), f32), vmem((2, width, width), f32)),
            sems((1,)), sems((APPLIES + 1,)),
            sems((chips,)), sems((2 * APPLIES + 1, chips)),
            sems((n_col,)), sems((2 * APPLIES + 1, n_col)),
            sems((chips,)), sems((APPLIES, chips)),
            sems((1,)), sems((4,)),
            sems((chips,)), sems((4, chips)),
            sems((n_col,)), sems((2, n_col)),
        ],
        compiler_params=pltpu.CompilerParams(
            collective_id=0, has_side_effects=True, vmem_limit_bytes=60 * 1024 * 1024),
        interpret=interpret,
    )(table, blocks, start)


def panels(s, e, lo, hi):
    sub = lax.broadcasted_iota(jnp.int32, (8, BS), 0)
    lane = lax.broadcasted_iota(jnp.int32, (8, BS), 1)

    def panel(k, c):
        first = pl.multiple_of(k * 8, 8)
        for m in range(2):
            r = s[m, pl.ds(first, 8), :]
            g = e[m, pl.ds(first, 8), :]
            own = jnp.where(lane >= first, jnp.where(lane < first + 8, r, 0.0), 0.0)
            cols = []
            for j in range(8):
                at_j = jnp.where(lane == first + j, own, 0.0)
                cols.append(jnp.broadcast_to(jnp.sum(at_j, axis=1, keepdims=True), (8, BS)))
            scale = jnp.zeros((8, BS), f32)
            for j in range(8):
                pivot = jnp.broadcast_to(cols[j][j:j + 1], (8, BS))
                mult = jnp.where(sub > j, cols[j] / pivot, 0.0)
                scale = jnp.where(sub == j, pivot, scale)
                r = r - mult * r[j:j + 1]
                g = g - mult * g[j:j + 1]
                for i in range(j + 1, 8):
                    cols[i] = cols[i] - mult * cols[i][j:j + 1]
            scale = 1.0 / jnp.sqrt(scale)
            v = r * scale
            g = g * scale
            e[m, pl.ds(first, 8), :] = g
            below = jnp.where(lane >= first + 8, v, 0.0)
            step = lax.dot_general(below, jnp.concatenate([v, g], axis=1), (((0,), (0,)), ((), ())),
                                   precision=highest, preferred_element_type=f32)
            s[m] -= step[:, :BS]
            e[m] -= step[:, BS:]
        return c
    lax.fori_loop(lo, hi, panel, 0)


def local(block_values, block_index, block_count, start_vectors, interpret=False):
    n_row = lax.axis_size("row")
    n_col = lax.axis_size("col")
    side = math.isqrt(n_row // 2)
    chips = side * side
    blocks = block_values[0, 0]
    slots = blocks.shape[0]
    first, second = block_index[0, 0, 0], block_index[0, 0, 1]
    owner = second // n_col
    place = (first % n_col) * n_row + (owner % 2) * chips + owner // 2
    slot_ids = jnp.arange(slots, dtype=jnp.int32)
    place = jnp.where(slot_ids < block_count[0, 0], place, -1)
    spots = jnp.arange(n_row * n_col, dtype=jnp.int32)
    table = jnp.sum(jnp.where(place[None, :] == spots[:, None], slot_ids[None, :] + 1, 0), axis=1)

    return fused(table, blocks, start_vectors, side, n_col, interpret)


def solution(mesh):
    return jax.shard_map(
        local,
        mesh=mesh,
        in_specs=(
            P("row", "col", None, None, None),
            P("row", "col", None, None),
            P("row", "col"),
            P(("row", "col"), None),
        ),
        out_specs=(P(("row", "col"), None), P(), P(("row", "col"), None), P()),
        check_vma=False,
    )
```

```python
import functools
import math

import jax
import jax.numpy as jnp
from jax import lax
from jax.experimental import pallas as pl
from jax.experimental.pallas import tpu as pltpu
from jax.sharding import PartitionSpec as P

APPLIES = 3
MESH = pl.DeviceIdType.MESH
highest = lax.Precision.HIGHEST
f32 = jnp.float32
bf16 = jnp.bfloat16
BS = 128


def kernel(side, n_col, width, table, stored, start, basis, projected, residual, scaled, scales,
           u, wt, wc, colp, colq, corep, rsend, rrecv, rowp, zsend, zrecv, yv, ytv,
           dacc, dcore, dxy, dz, gram_bufs, ritz_bufs, chol,
           s_core, r_core, s_xy, r_xy, s_z, r_z, s_fwd, r_fwd, s_rx, r_rx, s_rz, r_rz,
           t_core, q_core, t_xy, q_xy, t_z, q_z, blocks, b_sem):
    chips = side * side
    n_row = 2 * chips
    hw = width // 2
    row = lax.axis_index("row")
    z = lax.axis_index("col")
    core = lax.rem(row, 2)
    chip = row // 2
    y, x = chip // side, lax.rem(chip, side)
    other = 1 - core

    def sibling():
        return (chip * 2 + other, z)

    def xy_to(p):
        return lax.rem(y + p // side, side) * side + lax.rem(x + lax.rem(p, side), side)

    def xy_from(p):
        return lax.rem(y + side - p // side, side) * side + lax.rem(x + side - lax.rem(p, side), side)

    def z_to(p):
        return lax.rem(z + p, n_col)

    def z_from(p):
        return lax.rem(z + n_col - p, n_col)

    def xy_dev(t):
        return (t * 2 + core, z)

    def z_dev(t):
        return (row, t)

    def remote(src, dst, send, recv, dev):
        return pltpu.make_async_remote_copy(
            src_ref=src, dst_ref=dst, send_sem=send, recv_sem=recv,
            device_id=dev, device_id_type=MESH)

    def each(lo, hi, body, unroll=True):
        def step(i, c):
            body(i)
            return c
        lax.fori_loop(lo, hi, step, 0, unroll=unroll)

    load = pltpu.make_async_copy(stored, blocks, b_sem)
    load.start()

    barrier = pltpu.get_barrier_semaphore()
    pl.semaphore_signal(barrier, inc=1, device_id=sibling(), device_id_type=MESH)
    each(1, chips, lambda p: pl.semaphore_signal(
        barrier, inc=1, device_id=xy_dev(xy_to(p)), device_id_type=MESH))
    each(1, n_col, lambda p: pl.semaphore_signal(
        barrier, inc=1, device_id=z_dev(z_to(p)), device_id_type=MESH))

    dacc[...] = jnp.zeros_like(dacc)
    ones = jnp.ones((8, BS), f32)

    def fill_row(lr):
        def fill(pos, total):
            slot = table[lr * n_row + pos]
            live = (slot > 0).astype(f32)
            block = blocks[jnp.maximum(slot - 1, 0)].astype(f32) * live
            u[pl.ds(pl.multiple_of(lr * BS, BS), BS), pl.ds(pl.multiple_of(pos * BS, BS), BS)] = block.astype(bf16)
            size = jnp.abs(block)
            dacc[pos // chips, lax.rem(pos, chips)] += jnp.sum(size.reshape(BS // 8, 8, BS), axis=0)
            return total + size
        total = lax.fori_loop(0, n_row, fill, jnp.zeros((BS, BS), f32))
        rowp[0, lr, 0:8, 0:BS] = lax.dot_general(
            ones, total, (((1,), (1,)), ((), ())), precision=highest, preferred_element_type=f32)
    load.wait()
    each(0, n_col, fill_row, False)

    pl.semaphore_wait(barrier, 1 + (chips - 1) + (n_col - 1))

    D = APPLIES

    def deg_z(p, lr, slot):
        return remote(rowp.at[0, lr, 0:8, 0:BS], dz.at[p], s_z.at[p], r_z.at[D, p], z_dev(slot))
    each(1, n_col, lambda p: deg_z(p, z_to(p), z_to(p)).start())
    deg_core = remote(dacc.at[other], dcore, s_core.at[0], r_core.at[2 * D], sibling())
    deg_core.start()
    deg_core.wait()
    dacc[core] += dcore[...]

    def deg_xy(p):
        t = xy_to(p)
        return remote(dacc.at[core, t], dxy.at[p], s_xy.at[p], r_xy.at[D, p], xy_dev(t))
    each(1, chips, lambda p: deg_xy(p).start())
    dz[0] = rowp[0, z, 0:8, 0:BS]
    dxy[0] = dacc[core, chip]
    each(1, n_col, lambda p: deg_z(p, z_to(p), z_to(p)).wait())
    each(1, chips, lambda p: deg_xy(p).wait())
    degree = jnp.sum(dz[...], axis=0)[0:1] + jnp.sum(jnp.sum(dxy[...], axis=0), axis=0, keepdims=True)
    inv_row = 1.0 / jnp.sqrt(degree / BS + 1e-05)
    inv = jnp.broadcast_to(inv_row, (BS, BS)).T
    inv = inv[:, 0:1]
    yv[0] = start[...]

    def row_pos(k, t):
        return k * chips + t

    def apply_once(a, beside=lambda i: None):
        w = inv * yv[a]
        wc[(a % 2), pl.ds(pl.multiple_of(row_pos(core, chip) * BS, BS), BS), :] = w.astype(bf16)
        wt[a, :, pl.ds(pl.multiple_of(z * BS, BS), BS)] = w.T.astype(bf16)
        even = (a % 2)

        def wt_part(h, t):
            return wt.at[a, pl.ds(h * hw, hw), pl.ds(pl.multiple_of(t * BS, BS), BS)]

        def wc_part(h, k, t):
            return wc.at[even, pl.ds(pl.multiple_of(row_pos(k, t) * BS, BS), BS), pl.ds(h * hw, hw)]

        def z_send(h, p):
            part, i = wt_part(h, z), h * n_col + p
            return remote(part, part, s_z.at[i], r_z.at[a, i], z_dev(z_to(p)))

        def z_arrive(h, p):
            t, i = z_from(p), h * n_col + p
            return remote(wt_part(h, t), wt_part(h, t), s_z.at[i], r_z.at[a, i], z_dev(t))

        def xy_send(h, p):
            part, i = wc_part(h, core, chip), h * chips + p
            return remote(part, part, s_xy.at[i], r_xy.at[a, i], xy_dev(xy_to(p)))

        def xy_arrive(h, p):
            t, i = xy_from(p), h * chips + p
            return remote(wc_part(h, core, t), wc_part(h, core, t), s_xy.at[i], r_xy.at[a, i], xy_dev(t))

        def pass_on(h, k, p):
            t, i = xy_from(p), h * chips + p
            return remote(wc_part(h, k, t), wc_part(h, k, t), s_fwd.at[i], r_fwd.at[a, i], sibling())

        def swap(h):
            return remote(colq.at[h], corep.at[a, h], s_core.at[h], r_core.at[a * 2 + h], sibling())

        def rs_xy(h, p):
            i = h * chips + p
            return remote(rsend.at[h, p], rrecv.at[a, h, p], s_rx.at[i], r_rx.at[a, i], xy_dev(xy_to(p)))

        def rs_z(h, p):
            i = h * n_col + p
            return remote(zsend.at[h, p], zrecv.at[a, h, p], s_rz.at[i], r_rz.at[a, i], z_dev(z_to(p)))

        def send_out(h):
            each(1, n_col, lambda p: z_send(h, p).start())
            each(1, chips, lambda p: xy_send(h, p).start())
            pass_on(h, core, 0).start()

        send_out(0)
        beside(0)

        def col_tiles(h, k, out_ref):
            def tile(n):
                first = (k * chips + 2 * n) * BS
                out = jnp.dot(wt[a, h * hw:(h + 1) * hw, :], u[:, pl.ds(pl.multiple_of(first, 2 * BS), 2 * BS)],
                              preferred_element_type=f32)
                out_ref[h, 2 * n] = out[:, :BS].astype(out_ref.dtype)
                out_ref[h, 2 * n + 1] = out[:, BS:].astype(out_ref.dtype)
            each(0, chips // 2, tile)

        for h in range(2):
            each(1, n_col, lambda p: z_arrive(h, p).wait_recv())
            if h == 0:
                send_out(1)
                beside(1)
            col_tiles(h, other, colq)
            swap(h).start()
            col_tiles(h, core, colp)

            def relay(p):
                xy_arrive(h, p).wait_recv()
                pass_on(h, core, p).start()
            each(1, chips, relay)
            if h == 0:
                beside(2)
            swap(h).wait_recv()

            def combine(p):
                t = xy_to(p)
                rsend[h, p] = (colp[h, t] + corep[a, h, t].astype(f32)).astype(bf16)
                rs_xy(h, p).start()
            each(1, chips, combine)
            each(0, chips, lambda p: pass_on(h, other, p).wait_recv())

            def row_tile(n):
                out = jnp.dot(u[pl.ds(pl.multiple_of(n * 2 * BS, 2 * BS), 2 * BS), :],
                              wc[even, :, h * hw:(h + 1) * hw], preferred_element_type=f32)
                rowp[h, 2 * n] = out[:BS]
                rowp[h, 2 * n + 1] = out[BS:]
            each(0, n_col // 2, row_tile)

            def row_go(p):
                zsend[h, p] = rowp[h, z_to(p)].astype(bf16)
                rs_z(h, p).start()
            each(1, n_col, row_go)
            beside(3 + h)

        for h in range(2):
            def add_col(p, total):
                rs_xy(h, p).wait_recv()
                return total + rrecv[a, h, p].astype(f32)
            cols = lax.fori_loop(1, chips, add_col, colp[h, chip] + corep[a, h, chip].astype(f32))

            def add_row(p, total):
                rs_z(h, p).wait_recv()
                return total + zrecv[a, h, p].astype(f32)
            rows = lax.fori_loop(1, n_col, add_row, rowp[h, z])
            out = inv * (rows + cols.T)
            yv[a + 1, :, h * hw:(h + 1) * hw] = out
            ytv[a, h * hw:(h + 1) * hw, :] = out.T
        for h in range(2):
            swap(h).wait_send()

            def xy_sent(p):
                xy_send(h, p).wait_send()
                rs_xy(h, p).wait_send()
            each(1, chips, xy_sent)

            def z_sent(p):
                z_send(h, p).wait_send()
                rs_z(h, p).wait_send()
            each(1, n_col, z_sent)
            each(0, chips, lambda p: pass_on(h, core, p).wait_send())

    def local_gram(a, b, into, n):
        g = jnp.dot(ytv[a], yv[b], precision=highest, preferred_element_type=f32)
        g = g.reshape(2, chips, width // n_row, width)
        for k in range(2):
            for t in range(chips):
                into[k, t, n] = g[k, t]

    def sum_steps(bufs, base):
        gr, ga, gb, gc, gd = bufs
        q = 2 * base
        g_core = remote(gr.at[other], ga, t_core.at[0], q_core.at[q], sibling())
        g_last = remote(gd.at[core], gd.at[core], t_core.at[0], q_core.at[q + 1], sibling())

        def g_xy(p):
            t = xy_to(p)
            return remote(gr.at[core, t], gb.at[p], t_xy.at[p], q_xy.at[q, p], xy_dev(t))

        def g_z(p):
            return remote(gc.at[0], gc.at[p], t_z.at[p], q_z.at[base, p], z_dev(z_to(p)))

        def g_back(p):
            t = xy_from(p)
            return remote(gd.at[core, t], gd.at[core, t], t_xy.at[p], q_xy.at[q + 1, p], xy_dev(t))

        def g_out(p):
            return remote(gd.at[core, chip], gd.at[core, chip], t_xy.at[p], q_xy.at[q + 1, p], xy_dev(xy_to(p)))

        def add_z(t, total):
            return total + gc[lax.rem(z + n_col - t, n_col)]

        def step1():
            g_core.wait()
            gr[core] += ga[...]
            each(1, chips, lambda p: g_xy(p).start())

        def step2():
            each(1, chips, lambda p: g_xy(p).wait())
            gb[0] = gr[core, chip]
            gc[0] = jnp.sum(gb[...], axis=0)
            each(1, n_col, lambda p: g_z(p).start())

        def step3():
            each(1, n_col, lambda p: g_z(p).wait())
            gd[core, chip] = lax.fori_loop(1, n_col, add_z, gc[z])
            each(1, chips, lambda p: g_out(p).start())

        def step4():
            each(1, chips, lambda p: g_back(p).wait_recv())
            each(1, chips, lambda p: g_out(p).wait_send())
            g_last.start()

        def step5():
            g_last.wait_send()
            remote(gd.at[other], gd.at[other], t_core.at[0], q_core.at[q + 1], sibling()).wait_recv()

        return g_core.start, step1, step2, step3, step4, step5

    mul = functools.partial(jnp.dot, precision=highest, preferred_element_type=f32)
    tmul = lambda a, b: lax.dot_general(a, b, (((0,), (0,)), ((), ())), precision=highest, preferred_element_type=f32)
    s, e, li, half, full = chol

    gram_sum = sum_steps(gram_bufs, 0)

    def last_apply(i):
        if i == 0:
            local_gram(0, 1, gram_bufs[0], 0)
            local_gram(1, 2, gram_bufs[0], 1)
            gram_sum[0]()
            gram_sum[1]()
        else:
            gram_sum[i + 1]()
        if i == 4:
            first_factors()

    def first_factors():
        for m in range(2):
            full[m] = gram_bufs[4][:, :, m].reshape(width, width)
            s[m] = full[m, :BS, :BS]
        unit(e)
        panels(s, e, 0, BS // 8)
        for m in range(2):
            li[m, :BS, :BS] = e[m]
            li[m, :BS, BS:] = jnp.zeros((BS, BS), f32)
            half[m] = mul(e[m], full[m, :BS, BS:])
            s[m] = full[m, BS:, BS:] - tmul(half[m], half[m])
        unit(e)

    each(0, APPLIES - 1, apply_once, False)
    apply_once(APPLIES - 1, last_apply)
    local_gram(1, 3, ritz_bufs[0], 0)
    cuts = (0, 2, 7, 11, 16)

    def second_factors(i):
        if i < 4:
            panels(s, e, cuts[i], cuts[i + 1])
        else:
            for m in range(2):
                li[m, BS:, BS:] = e[m]
                li[m, BS:, :BS] = -mul(e[m], tmul(half[m], li[m, :BS, :BS]))
            gram = mul(mul(li[0], full[1]), li[0].T)
            scaled[...] = gram
            scales[1] = jnp.broadcast_to(
                1.0 / jnp.sqrt(jnp.sum(gram * gram, keepdims=True) / (width * width) + 1e-06), (8, BS))
            full[0] = li[1].T
            yv[0] = mul(yv[2], full[0])
            yv[1] = mul(yv[3], full[0])

    ritz_sum = sum_steps(ritz_bufs, 1)
    for i in range(5):
        ritz_sum[i]()
        second_factors(i)
    ritz_sum[5]()
    ritz = mul(mul(li[1], ritz_bufs[4][:, :, 0].reshape(width, width)), full[0])
    scales[0] = jnp.broadcast_to(1.0 / jnp.sqrt(jnp.sum(ritz * ritz, keepdims=True) / (width * width) + 1e-06), (8, BS))
    projected[...] = ritz
    basis[...] = yv[0]
    residual[...] = yv[1] - mul(yv[0], ritz)


def unit(e):
    eye = (lax.broadcasted_iota(jnp.int32, (BS, BS), 0) == lax.broadcasted_iota(jnp.int32, (BS, BS), 1)).astype(f32)
    for m in range(2):
        e[m] = eye


def fused(table, blocks, start, side, n_col, interpret=False):
    chips = side * side
    n_row = 2 * chips
    width = start.shape[1]
    sems = pltpu.SemaphoreType.DMA
    vmem = pltpu.VMEM
    part = width // n_row
    hw = width // 2
    tall = jax.ShapeDtypeStruct((BS, width), f32)
    square = jax.ShapeDtypeStruct((width, width), f32)

    def sum_bufs(n):
        return (vmem((2, chips, n, part, width), f32), vmem((chips, n, part, width), f32),
                vmem((chips, n, part, width), f32), vmem((n_col, n, part, width), f32),
                vmem((2, chips, n, part, width), f32))
    return pl.pallas_call(
        functools.partial(kernel, side, n_col, width),
        out_shape=(tall, square, tall, square, jax.ShapeDtypeStruct((2, 8, BS), f32)),
        in_specs=[pl.BlockSpec(memory_space=pltpu.SMEM), pl.BlockSpec(memory_space=pl.ANY), pl.BlockSpec(memory_space=pltpu.VMEM)],
        out_specs=tuple([pl.BlockSpec(memory_space=pltpu.VMEM)] * 5),
        scratch_shapes=[
            vmem((n_col * BS, n_row * BS), bf16),
            vmem((APPLIES, width, n_col * BS), bf16),
            vmem((2, n_row * BS, width), bf16),
            vmem((2, chips, hw, BS), f32),
            vmem((2, chips, hw, BS), bf16),
            vmem((APPLIES, 2, chips, hw, BS), bf16),
            vmem((2, chips, hw, BS), bf16),
            vmem((APPLIES, 2, chips, hw, BS), bf16),
            vmem((2, n_col, BS, hw), f32),
            vmem((2, n_col, BS, hw), bf16),
            vmem((APPLIES, 2, n_col, BS, hw), bf16),
            vmem((APPLIES + 1, BS, width), f32),
            vmem((APPLIES, width, BS), f32),
            vmem((2, chips, 8, BS), f32),
            vmem((chips, 8, BS), f32),
            vmem((chips, 8, BS), f32),
            vmem((n_col, 8, BS), f32),
            sum_bufs(2), sum_bufs(1),
            (vmem((2, BS, BS), f32), vmem((2, BS, BS), f32), vmem((2, width, width), f32),
             vmem((2, BS, BS), f32), vmem((2, width, width), f32)),
            sems((2,)), sems((2 * APPLIES + 1,)),
            sems((2 * chips,)), sems((APPLIES + 1, 2 * chips)),
            sems((2 * n_col,)), sems((APPLIES + 1, 2 * n_col)),
            sems((2 * chips,)), sems((APPLIES, 2 * chips)),
            sems((2 * chips,)), sems((APPLIES, 2 * chips)),
            sems((2 * n_col,)), sems((APPLIES, 2 * n_col)),
            sems((1,)), sems((4,)),
            sems((chips,)), sems((4, chips)),
            sems((n_col,)), sems((2, n_col)),
            vmem(blocks.shape, bf16), sems(()),
        ],
        compiler_params=pltpu.CompilerParams(
            collective_id=0, has_side_effects=True, vmem_limit_bytes=60 * 1024 * 1024),
        interpret=interpret,
    )(table, blocks, start)


def panels(s, e, lo, hi):
    sub = lax.broadcasted_iota(jnp.int32, (8, BS), 0)
    lane = lax.broadcasted_iota(jnp.int32, (8, BS), 1)

    def panel(k, c):
        first = pl.multiple_of(k * 8, 8)
        for m in range(2):
            r = s[m, pl.ds(first, 8), :]
            g = e[m, pl.ds(first, 8), :]
            own = jnp.where(lane >= first, jnp.where(lane < first + 8, r, 0.0), 0.0)
            cols = []
            for j in range(8):
                at_j = jnp.where(lane == first + j, own, 0.0)
                cols.append(jnp.broadcast_to(jnp.sum(at_j, axis=1, keepdims=True), (8, BS)))
            scale = jnp.zeros((8, BS), f32)
            for j in range(8):
                pivot = jnp.broadcast_to(cols[j][j:j + 1], (8, BS))
                mult = jnp.where(sub > j, cols[j] / pivot, 0.0)
                scale = jnp.where(sub == j, pivot, scale)
                r = r - mult * r[j:j + 1]
                g = g - mult * g[j:j + 1]
                for i in range(j + 1, 8):
                    cols[i] = cols[i] - mult * cols[i][j:j + 1]
            scale = 1.0 / jnp.sqrt(scale)
            v = r * scale
            g = g * scale
            e[m, pl.ds(first, 8), :] = g
            below = jnp.where(lane >= first + 8, v, 0.0)
            step = lax.dot_general(below, jnp.concatenate([v, g], axis=1), (((0,), (0,)), ((), ())),
                                   precision=highest, preferred_element_type=f32)
            s[m] -= step[:, :BS]
            e[m] -= step[:, BS:]
        return c
    lax.fori_loop(lo, hi, panel, 0)


def local(block_values, block_index, block_count, start_vectors, interpret=False):
    n_row = lax.axis_size("row")
    n_col = lax.axis_size("col")
    side = math.isqrt(n_row // 2)
    chips = side * side
    blocks = block_values[0, 0]
    slots = blocks.shape[0]
    first, second = block_index[0, 0, 0], block_index[0, 0, 1]
    owner = second // n_col
    place = (first % n_col) * n_row + (owner % 2) * chips + owner // 2
    slot_ids = jnp.arange(slots, dtype=jnp.int32)
    place = jnp.where(slot_ids < block_count[0, 0], place, -1)
    spots = jnp.arange(n_row * n_col, dtype=jnp.int32)
    table = jnp.sum(jnp.where(place[None, :] == spots[:, None], slot_ids[None, :] + 1, 0), axis=1)

    parts = fused(table, blocks, start_vectors, side, n_col, interpret)
    total_rows = BS * n_row * n_col
    whole = pl.BlockSpec(memory_space=pltpu.VMEM)
    return pl.pallas_call(
        functools.partial(scale_kernel, math.sqrt(total_rows), math.sqrt(total_rows / start_vectors.shape[1])),
        out_shape=tuple(jax.ShapeDtypeStruct(p.shape, f32) for p in parts[:4]),
        in_specs=[whole] * 5,
        out_specs=(whole,) * 4,
        interpret=interpret,
    )(*parts)


def scale_kernel(tall, rest, subspace, ritz, residual, gram, scales, basis, projected, ritz_residual, gram_scaled):
    inverse_spread, inverse_size = scales[0, 0:1, 0:1], scales[1, 0:1, 0:1]
    basis[...] = subspace[...] * tall
    projected[...] = ritz[...] * inverse_spread
    ritz_residual[...] = residual[...] * (inverse_spread * rest)
    gram_scaled[...] = gram[...] * inverse_size


def solution(mesh):
    return jax.shard_map(
        local,
        mesh=mesh,
        in_specs=(
            P("row", "col", None, None, None),
            P("row", "col", None, None),
            P("row", "col"),
            P(("row", "col"), None),
        ),
        out_specs=(P(("row", "col"), None), P(), P(("row", "col"), None), P()),
        check_vma=False,
    )
```

```python
import functools
import math

import jax
import jax.numpy as jnp
from jax import lax
from jax.experimental import pallas as pl
from jax.experimental.pallas import tpu as pltpu
from jax.sharding import PartitionSpec as P

APPLIES = 3
MESH = pl.DeviceIdType.MESH
highest = lax.Precision.HIGHEST
f32 = jnp.float32
bf16 = jnp.bfloat16
BS = 128


def kernel(side, n_col, width, table, stored, start, basis, projected, residual, scaled, scales,
           u, wt, wc, colp, colq, corep, rsend, rrecv, rowp, zsend, zrecv, yv, ytv,
           dacc, dcore, dxy, dz, gram_bufs, ritz_bufs, chol,
           s_core, r_core, s_xy, r_xy, s_z, r_z, s_fwd, r_fwd, s_rx, r_rx, s_rz, r_rz,
           t_core, q_core, t_xy, q_xy, t_z, q_z, blocks, b_sem):
    chips = side * side
    n_row = 2 * chips
    hw = width // 2
    row = lax.axis_index("row")
    z = lax.axis_index("col")
    core = lax.rem(row, 2)
    chip = row // 2
    y, x = chip // side, lax.rem(chip, side)
    other = 1 - core

    def sibling():
        return (chip * 2 + other, z)

    def xy_to(p):
        return lax.rem(y + p // side, side) * side + lax.rem(x + lax.rem(p, side), side)

    def xy_from(p):
        return lax.rem(y + side - p // side, side) * side + lax.rem(x + side - lax.rem(p, side), side)

    def z_to(p):
        return lax.rem(z + p, n_col)

    def z_from(p):
        return lax.rem(z + n_col - p, n_col)

    def xy_dev(t):
        return (t * 2 + core, z)

    def z_dev(t):
        return (row, t)

    def remote(src, dst, send, recv, dev):
        return pltpu.make_async_remote_copy(
            src_ref=src, dst_ref=dst, send_sem=send, recv_sem=recv,
            device_id=dev, device_id_type=MESH)

    def each(lo, hi, body, unroll=True):
        def step(i, c):
            body(i)
            return c
        lax.fori_loop(lo, hi, step, 0, unroll=unroll)

    load = pltpu.make_async_copy(stored, blocks, b_sem)
    load.start()

    barrier = pltpu.get_barrier_semaphore()
    pl.semaphore_signal(barrier, inc=1, device_id=sibling(), device_id_type=MESH)
    each(1, chips, lambda p: pl.semaphore_signal(
        barrier, inc=1, device_id=xy_dev(xy_to(p)), device_id_type=MESH))
    each(1, n_col, lambda p: pl.semaphore_signal(
        barrier, inc=1, device_id=z_dev(z_to(p)), device_id_type=MESH))

    dacc[...] = jnp.zeros_like(dacc)
    ones = jnp.ones((8, BS), f32)

    def fill_row(lr):
        def fill(pos, total):
            slot = table[lr * n_row + pos]
            live = (slot > 0).astype(f32)
            block = blocks[jnp.maximum(slot - 1, 0)].astype(f32) * live
            u[pl.ds(pl.multiple_of(lr * BS, BS), BS), pl.ds(pl.multiple_of(pos * BS, BS), BS)] = block.astype(bf16)
            size = jnp.abs(block)
            dacc[pos // chips, lax.rem(pos, chips)] += jnp.sum(size.reshape(BS // 8, 8, BS), axis=0)
            return total + size
        total = lax.fori_loop(0, n_row, fill, jnp.zeros((BS, BS), f32))
        rowp[0, lr, 0:8, 0:BS] = lax.dot_general(
            ones, total, (((1,), (1,)), ((), ())), precision=highest, preferred_element_type=f32)
    load.wait()
    each(0, n_col, fill_row, False)

    pl.semaphore_wait(barrier, 1 + (chips - 1) + (n_col - 1))

    D = APPLIES

    def deg_z(p, lr, slot):
        return remote(rowp.at[0, lr, 0:8, 0:BS], dz.at[p], s_z.at[0], r_z.at[D, 0], z_dev(slot))
    each(1, n_col, lambda p: deg_z(p, z_to(p), z_to(p)).start())
    deg_core = remote(dacc.at[other], dcore, s_core.at[0], r_core.at[2 * D], sibling())
    deg_core.start()
    deg_core.wait()
    dacc[core] += dcore[...]

    def deg_xy(p):
        t = xy_to(p)
        return remote(dacc.at[core, t], dxy.at[p], s_xy.at[0], r_xy.at[D, 0], xy_dev(t))
    each(1, chips, lambda p: deg_xy(p).start())
    dz[0] = rowp[0, z, 0:8, 0:BS]
    dxy[0] = dacc[core, chip]
    remote(dz.at[1:], dz.at[1:], s_z.at[0], r_z.at[D, 0], z_dev(z_to(1))).wait()
    remote(dxy.at[1:], dxy.at[1:], s_xy.at[0], r_xy.at[D, 0], xy_dev(xy_to(1))).wait()
    degree = jnp.sum(dz[...], axis=0)[0:1] + jnp.sum(jnp.sum(dxy[...], axis=0), axis=0, keepdims=True)
    inv_row = 1.0 / jnp.sqrt(degree / BS + 1e-05)
    inv = jnp.broadcast_to(inv_row, (BS, BS)).T
    inv = inv[:, 0:1]
    yv[0] = start[...]

    def row_pos(k, t):
        return k * chips + t

    def apply_once(a, beside=lambda i: None):
        w = inv * yv[a]
        wc[(a % 2), pl.ds(pl.multiple_of(row_pos(core, chip) * BS, BS), BS), :] = w.astype(bf16)
        wt[a, :, pl.ds(pl.multiple_of(z * BS, BS), BS)] = w.T.astype(bf16)
        even = (a % 2)

        def wt_part(h, t):
            return wt.at[a, pl.ds(h * hw, hw), pl.ds(pl.multiple_of(t * BS, BS), BS)]

        def wc_part(h, k, t):
            return wc.at[even, pl.ds(pl.multiple_of(row_pos(k, t) * BS, BS), BS), pl.ds(h * hw, hw)]

        def z_send(h, p):
            return remote(wt_part(h, z), wt_part(h, z), s_z.at[h], r_z.at[a, h], z_dev(z_to(p)))

        def xy_send(h, p):
            part = wc_part(h, core, chip)
            return remote(part, part, s_xy.at[h], r_xy.at[a, h], xy_dev(xy_to(p)))

        def z_all(h):
            return remote(zsend.at[h, 1:], zrecv.at[a, h, 1:], s_z.at[h], r_z.at[a, h], z_dev(z_to(1)))

        def xy_all(h):
            return remote(rsend.at[h, 1:], rrecv.at[a, h, 1:], s_xy.at[h], r_xy.at[a, h], xy_dev(xy_to(1)))

        def rs_z_all(h):
            return remote(zsend.at[h, 1:], zrecv.at[a, h, 1:], s_rz.at[h], r_rz.at[a, h], z_dev(z_to(1)))

        def rs_xy_all(h):
            return remote(rsend.at[h, 1:], rrecv.at[a, h, 1:], s_rx.at[h], r_rx.at[a, h], xy_dev(xy_to(1)))

        def pass_on(h, k, g):
            first = row_pos(k, g * side) * BS
            part = wc.at[even, pl.ds(pl.multiple_of(first, BS), side * BS), pl.ds(h * hw, hw)]
            return remote(part, part, s_fwd.at[h, g], r_fwd.at[a, h * side + g], sibling())

        def swap(h):
            return remote(colq.at[h], corep.at[a, h], s_core.at[h], r_core.at[a * 2 + h], sibling())

        def rs_xy(h, p):
            return remote(rsend.at[h, p], rrecv.at[a, h, p], s_rx.at[h], r_rx.at[a, h], xy_dev(xy_to(p)))

        def rs_z(h, p):
            return remote(zsend.at[h, p], zrecv.at[a, h, p], s_rz.at[h], r_rz.at[a, h], z_dev(z_to(p)))

        def send_out(h):
            each(1, n_col, lambda p: z_send(h, p).start())
            each(1, chips, lambda p: xy_send(h, p).start())

        send_out(0)
        beside(0)

        def col_tiles(h, k, out_ref):
            def tile(n):
                first = (k * chips + 2 * n) * BS
                out = jnp.dot(wt[a, h * hw:(h + 1) * hw, :], u[:, pl.ds(pl.multiple_of(first, 2 * BS), 2 * BS)],
                              preferred_element_type=f32)
                out_ref[h, 2 * n] = out[:, :BS].astype(out_ref.dtype)
                out_ref[h, 2 * n + 1] = out[:, BS:].astype(out_ref.dtype)
            each(0, chips // 2, tile)

        for h in range(2):
            z_all(h).wait_recv()
            if h == 0:
                send_out(1)
                beside(1)
            col_tiles(h, other, colq)
            swap(h).start()
            col_tiles(h, core, colp)
            xy_all(h).wait_recv()
            each(0, side, lambda g: pass_on(h, core, g).start())
            if h == 0:
                beside(2)
            swap(h).wait_recv()

            def combine(p):
                t = xy_to(p)
                rsend[h, p] = (colp[h, t] + corep[a, h, t].astype(f32)).astype(bf16)
                rs_xy(h, p).start()
            each(1, chips, combine)
            each(0, side, lambda g: pass_on(h, other, g).wait_recv())

            def row_tile(n):
                out = jnp.dot(u[pl.ds(pl.multiple_of(n * 2 * BS, 2 * BS), 2 * BS), :],
                              wc[even, :, h * hw:(h + 1) * hw], preferred_element_type=f32)
                rowp[h, 2 * n] = out[:BS]
                rowp[h, 2 * n + 1] = out[BS:]
            each(0, n_col // 2, row_tile)

            def row_go(p):
                zsend[h, p] = rowp[h, z_to(p)].astype(bf16)
                rs_z(h, p).start()
            each(1, n_col, row_go)
            beside(3 + h)

        for h in range(2):
            rs_xy_all(h).wait_recv()
            cols = colp[h, chip] + corep[a, h, chip].astype(f32)
            for p in range(1, chips):
                cols = cols + rrecv[a, h, p].astype(f32)
            rs_z_all(h).wait_recv()
            rows = rowp[h, z]
            for p in range(1, n_col):
                rows = rows + zrecv[a, h, p].astype(f32)
            out = inv * (rows + cols.T)
            yv[a + 1, :, h * hw:(h + 1) * hw] = out
            ytv[a, h * hw:(h + 1) * hw, :] = out.T
        for h in range(2):
            swap(h).wait_send()
            for copies in (z_all(h), xy_all(h), rs_z_all(h), rs_xy_all(h)):
                copies.wait_send()
            each(0, side, lambda g: pass_on(h, core, g).wait_send())

    def local_gram(a, b, into, n):
        g = jnp.dot(ytv[a], yv[b], precision=highest, preferred_element_type=f32)
        g = g.reshape(2, chips, width // n_row, width)
        for k in range(2):
            for t in range(chips):
                into[k, t, n] = g[k, t]

    def sum_steps(bufs, base):
        gr, ga, gb, gc, gd = bufs
        q = 2 * base
        g_core = remote(gr.at[other], ga, t_core.at[0], q_core.at[q], sibling())
        g_last = remote(gd.at[core], gd.at[core], t_core.at[0], q_core.at[q + 1], sibling())

        def g_xy(p):
            t = xy_to(p)
            return remote(gr.at[core, t], gb.at[p], t_xy.at[q], q_xy.at[q], xy_dev(t))

        def g_z(p):
            return remote(gc.at[0], gc.at[p], t_z.at[base], q_z.at[base], z_dev(z_to(p)))

        def all_xy(k):
            return remote(ga.at[1:], gb.at[1:], t_xy.at[k], q_xy.at[k], xy_dev(xy_to(1)))

        def g_out(p):
            return remote(gd.at[core, chip], gd.at[core, chip], t_xy.at[q + 1], q_xy.at[q + 1], xy_dev(xy_to(p)))

        def add_z(t, total):
            return total + gc[lax.rem(z + n_col - t, n_col)]

        def step1():
            g_core.wait()
            gr[core] += ga[...]
            each(1, chips, lambda p: g_xy(p).start())

        def step2():
            all_xy(q).wait()
            gb[0] = gr[core, chip]
            gc[0] = jnp.sum(gb[...], axis=0)
            each(1, n_col, lambda p: g_z(p).start())

        def step3():
            remote(gc.at[1:], gc.at[1:], t_z.at[base], q_z.at[base], z_dev(z_to(1))).wait()
            gd[core, chip] = lax.fori_loop(1, n_col, add_z, gc[z])
            each(1, chips, lambda p: g_out(p).start())

        def step4():
            all_xy(q + 1).wait()
            g_last.start()

        def step5():
            g_last.wait_send()
            remote(gd.at[other], gd.at[other], t_core.at[0], q_core.at[q + 1], sibling()).wait_recv()

        return g_core.start, step1, step2, step3, step4, step5

    mul = functools.partial(jnp.dot, precision=highest, preferred_element_type=f32)
    tmul = lambda a, b: lax.dot_general(a, b, (((0,), (0,)), ((), ())), precision=highest, preferred_element_type=f32)
    s, e, li, half, full = chol

    gram_sum = sum_steps(gram_bufs, 0)

    def last_apply(i):
        if i == 0:
            local_gram(0, 1, gram_bufs[0], 0)
            local_gram(1, 2, gram_bufs[0], 1)
            gram_sum[0]()
            gram_sum[1]()
        else:
            gram_sum[i + 1]()
        if i == 4:
            first_factors()

    def first_factors():
        for m in range(2):
            full[m] = gram_bufs[4][:, :, m].reshape(width, width)
            s[m] = full[m, :BS, :BS]
        unit(e)
        panels(s, e, 0, BS // 8)
        for m in range(2):
            li[m, :BS, :BS] = e[m]
            li[m, :BS, BS:] = jnp.zeros((BS, BS), f32)
            half[m] = mul(e[m], full[m, :BS, BS:])
            s[m] = full[m, BS:, BS:] - tmul(half[m], half[m])
        unit(e)

    each(0, APPLIES - 1, apply_once, False)
    apply_once(APPLIES - 1, last_apply)
    local_gram(1, 3, ritz_bufs[0], 0)
    cuts = (0, 2, 7, 11, 16)

    def second_factors(i):
        if i < 4:
            panels(s, e, cuts[i], cuts[i + 1])
        else:
            for m in range(2):
                li[m, BS:, BS:] = e[m]
                li[m, BS:, :BS] = -mul(e[m], tmul(half[m], li[m, :BS, :BS]))
            gram = mul(mul(li[0], full[1]), li[0].T)
            scaled[...] = gram
            scales[1] = jnp.broadcast_to(
                1.0 / jnp.sqrt(jnp.sum(gram * gram, keepdims=True) / (width * width) + 1e-06), (8, BS))
            full[0] = li[1].T
            yv[0] = mul(yv[2], full[0])
            yv[1] = mul(yv[3], full[0])

    ritz_sum = sum_steps(ritz_bufs, 1)
    for i in range(5):
        ritz_sum[i]()
        second_factors(i)
    ritz_sum[5]()
    ritz = mul(mul(li[1], ritz_bufs[4][:, :, 0].reshape(width, width)), full[0])
    scales[0] = jnp.broadcast_to(1.0 / jnp.sqrt(jnp.sum(ritz * ritz, keepdims=True) / (width * width) + 1e-06), (8, BS))
    projected[...] = ritz
    basis[...] = yv[0]
    residual[...] = yv[1] - mul(yv[0], ritz)


def unit(e):
    eye = (lax.broadcasted_iota(jnp.int32, (BS, BS), 0) == lax.broadcasted_iota(jnp.int32, (BS, BS), 1)).astype(f32)
    for m in range(2):
        e[m] = eye


def fused(table, blocks, start, side, n_col, interpret=False):
    chips = side * side
    n_row = 2 * chips
    width = start.shape[1]
    sems = pltpu.SemaphoreType.DMA
    vmem = pltpu.VMEM
    part = width // n_row
    hw = width // 2
    tall = jax.ShapeDtypeStruct((BS, width), f32)
    square = jax.ShapeDtypeStruct((width, width), f32)

    def sum_bufs(n):
        return (vmem((2, chips, n, part, width), f32), vmem((chips, n, part, width), f32),
                vmem((chips, n, part, width), f32), vmem((n_col, n, part, width), f32),
                vmem((2, chips, n, part, width), f32))
    return pl.pallas_call(
        functools.partial(kernel, side, n_col, width),
        out_shape=(tall, square, tall, square, jax.ShapeDtypeStruct((2, 8, BS), f32)),
        in_specs=[pl.BlockSpec(memory_space=pltpu.SMEM), pl.BlockSpec(memory_space=pl.ANY), pl.BlockSpec(memory_space=pltpu.VMEM)],
        out_specs=tuple([pl.BlockSpec(memory_space=pltpu.VMEM)] * 5),
        scratch_shapes=[
            vmem((n_col * BS, n_row * BS), bf16),
            vmem((APPLIES, width, n_col * BS), bf16),
            vmem((2, n_row * BS, width), bf16),
            vmem((2, chips, hw, BS), f32),
            vmem((2, chips, hw, BS), bf16),
            vmem((APPLIES, 2, chips, hw, BS), bf16),
            vmem((2, chips, hw, BS), bf16),
            vmem((APPLIES, 2, chips, hw, BS), bf16),
            vmem((2, n_col, BS, hw), f32),
            vmem((2, n_col, BS, hw), bf16),
            vmem((APPLIES, 2, n_col, BS, hw), bf16),
            vmem((APPLIES + 1, BS, width), f32),
            vmem((APPLIES, width, BS), f32),
            vmem((2, chips, 8, BS), f32),
            vmem((chips, 8, BS), f32),
            vmem((chips, 8, BS), f32),
            vmem((n_col, 8, BS), f32),
            sum_bufs(2), sum_bufs(1),
            (vmem((2, BS, BS), f32), vmem((2, BS, BS), f32), vmem((2, width, width), f32),
             vmem((2, BS, BS), f32), vmem((2, width, width), f32)),
            sems((2,)), sems((2 * APPLIES + 1,)),
            sems((2,)), sems((APPLIES + 1, 2)),
            sems((2,)), sems((APPLIES + 1, 2)),
            sems((2, side)), sems((APPLIES, 2 * side)),
            sems((2,)), sems((APPLIES, 2)),
            sems((2,)), sems((APPLIES, 2)),
            sems((1,)), sems((4,)),
            sems((4,)), sems((4,)),
            sems((2,)), sems((2,)),
            vmem(blocks.shape, bf16), sems(()),
        ],
        compiler_params=pltpu.CompilerParams(
            collective_id=0, has_side_effects=True, vmem_limit_bytes=60 * 1024 * 1024),
        interpret=interpret,
    )(table, blocks, start)


def panels(s, e, lo, hi):
    sub = lax.broadcasted_iota(jnp.int32, (8, BS), 0)
    lane = lax.broadcasted_iota(jnp.int32, (8, BS), 1)

    def panel(k, c):
        first = pl.multiple_of(k * 8, 8)
        for m in range(2):
            r = s[m, pl.ds(first, 8), :]
            g = e[m, pl.ds(first, 8), :]
            own = jnp.where(lane >= first, jnp.where(lane < first + 8, r, 0.0), 0.0)
            cols = []
            for j in range(8):
                at_j = jnp.where(lane == first + j, own, 0.0)
                cols.append(jnp.broadcast_to(jnp.sum(at_j, axis=1, keepdims=True), (8, BS)))
            scale = jnp.zeros((8, BS), f32)
            for j in range(8):
                pivot = jnp.broadcast_to(cols[j][j:j + 1], (8, BS))
                mult = jnp.where(sub > j, cols[j] / pivot, 0.0)
                scale = jnp.where(sub == j, pivot, scale)
                r = r - mult * r[j:j + 1]
                g = g - mult * g[j:j + 1]
                for i in range(j + 1, 8):
                    cols[i] = cols[i] - mult * cols[i][j:j + 1]
            scale = 1.0 / jnp.sqrt(scale)
            v = r * scale
            g = g * scale
            e[m, pl.ds(first, 8), :] = g
            below = jnp.where(lane >= first + 8, v, 0.0)
            step = lax.dot_general(below, jnp.concatenate([v, g], axis=1), (((0,), (0,)), ((), ())),
                                   precision=highest, preferred_element_type=f32)
            s[m] -= step[:, :BS]
            e[m] -= step[:, BS:]
        return c
    lax.fori_loop(lo, hi, panel, 0)


def local(block_values, block_index, block_count, start_vectors, interpret=False):
    n_row = lax.axis_size("row")
    n_col = lax.axis_size("col")
    side = math.isqrt(n_row // 2)
    chips = side * side
    blocks = block_values[0, 0]
    slots = blocks.shape[0]
    first, second = block_index[0, 0, 0], block_index[0, 0, 1]
    owner = second // n_col
    place = (first % n_col) * n_row + (owner % 2) * chips + owner // 2
    slot_ids = jnp.arange(slots, dtype=jnp.int32)
    place = jnp.where(slot_ids < block_count[0, 0], place, -1)
    spots = jnp.arange(n_row * n_col, dtype=jnp.int32)
    table = jnp.sum(jnp.where(place[None, :] == spots[:, None], slot_ids[None, :] + 1, 0), axis=1)

    parts = fused(table, blocks, start_vectors, side, n_col, interpret)
    total_rows = BS * n_row * n_col
    whole = pl.BlockSpec(memory_space=pltpu.VMEM)
    return pl.pallas_call(
        functools.partial(scale_kernel, math.sqrt(total_rows), math.sqrt(total_rows / start_vectors.shape[1])),
        out_shape=tuple(jax.ShapeDtypeStruct(p.shape, f32) for p in parts[:4]),
        in_specs=[whole] * 5,
        out_specs=(whole,) * 4,
        interpret=interpret,
    )(*parts)


def scale_kernel(tall, rest, subspace, ritz, residual, gram, scales, basis, projected, ritz_residual, gram_scaled):
    inverse_spread, inverse_size = scales[0, 0:1, 0:1], scales[1, 0:1, 0:1]
    basis[...] = subspace[...] * tall
    projected[...] = ritz[...] * inverse_spread
    ritz_residual[...] = residual[...] * (inverse_spread * rest)
    gram_scaled[...] = gram[...] * inverse_size


def solution(mesh):
    return jax.shard_map(
        local,
        mesh=mesh,
        in_specs=(
            P("row", "col", None, None, None),
            P("row", "col", None, None),
            P("row", "col"),
            P(("row", "col"), None),
        ),
        out_specs=(P(("row", "col"), None), P(), P(("row", "col"), None), P()),
        check_vma=False,
    )
```

```python
import functools
import math

import jax
import jax.numpy as jnp
from jax import lax
from jax.experimental import pallas as pl
from jax.experimental.pallas import tpu as pltpu
from jax.sharding import PartitionSpec as P

APPLIES = 3
MESH = pl.DeviceIdType.MESH
highest = lax.Precision.HIGHEST
f32 = jnp.float32
bf16 = jnp.bfloat16
BS = 128


def kernel(side, n_col, width, table, stored, start, basis, projected, residual, scaled, scales,
           u, wt, wc, colp, colq, corep, rsend, rrecv, rowp, zsend, zrecv, yv, ytv,
           dacc, dcore, dxy, dz, gram_bufs, ritz_bufs, chol,
           s_core, r_core, s_xy, r_xy, s_z, r_z, s_fwd, r_fwd, s_rx, r_rx, s_rz, r_rz,
           t_core, q_core, t_xy, q_xy, t_z, q_z, blocks, b_sem):
    chips = side * side
    n_row = 2 * chips
    hw = width // 2
    row = lax.axis_index("row")
    z = lax.axis_index("col")
    core = lax.rem(row, 2)
    chip = row // 2
    y, x = chip // side, lax.rem(chip, side)
    other = 1 - core

    def sibling():
        return (chip * 2 + other, z)

    def xy_to(p):
        return lax.rem(y + p // side, side) * side + lax.rem(x + lax.rem(p, side), side)

    def xy_from(p):
        return lax.rem(y + side - p // side, side) * side + lax.rem(x + side - lax.rem(p, side), side)

    def z_to(p):
        return lax.rem(z + p, n_col)

    def z_from(p):
        return lax.rem(z + n_col - p, n_col)

    def xy_dev(t):
        return (t * 2 + core, z)

    def z_dev(t):
        return (row, t)

    def remote(src, dst, send, recv, dev):
        return pltpu.make_async_remote_copy(
            src_ref=src, dst_ref=dst, send_sem=send, recv_sem=recv,
            device_id=dev, device_id_type=MESH)

    def each(lo, hi, body, unroll=True):
        def step(i, c):
            body(i)
            return c
        lax.fori_loop(lo, hi, step, 0, unroll=unroll)

    load = pltpu.make_async_copy(stored, blocks, b_sem)
    load.start()

    barrier = pltpu.get_barrier_semaphore()
    pl.semaphore_signal(barrier, inc=1, device_id=sibling(), device_id_type=MESH)
    each(1, chips, lambda p: pl.semaphore_signal(
        barrier, inc=1, device_id=xy_dev(xy_to(p)), device_id_type=MESH))
    each(1, n_col, lambda p: pl.semaphore_signal(
        barrier, inc=1, device_id=z_dev(z_to(p)), device_id_type=MESH))

    dacc[...] = jnp.zeros_like(dacc)
    ones = jnp.ones((8, BS), f32)

    def fill_row(lr):
        def fill(pos, total):
            slot = table[lr * n_row + pos]
            live = (slot > 0).astype(f32)
            block = blocks[jnp.maximum(slot - 1, 0)].astype(f32) * live
            u[pl.ds(pl.multiple_of(lr * BS, BS), BS), pl.ds(pl.multiple_of(pos * BS, BS), BS)] = block.astype(bf16)
            size = jnp.abs(block)
            dacc[pos // chips, lax.rem(pos, chips)] += jnp.sum(size.reshape(BS // 8, 8, BS), axis=0)
            return total + size
        total = lax.fori_loop(0, n_row, fill, jnp.zeros((BS, BS), f32))
        rowp[0, lr, 0:8, 0:BS] = lax.dot_general(
            ones, total, (((1,), (1,)), ((), ())), precision=highest, preferred_element_type=f32)
    load.wait()
    each(0, n_col, fill_row, False)

    pl.semaphore_wait(barrier, 1 + (chips - 1) + (n_col - 1))

    D = APPLIES

    def deg_z(p, lr, slot):
        return remote(rowp.at[0, lr, 0:8, 0:BS], dz.at[p], s_z.at[0], r_z.at[D, 0], z_dev(slot))
    each(1, n_col, lambda p: deg_z(p, z_to(p), z_to(p)).start())
    deg_core = remote(dacc.at[other], dcore, s_core.at[0], r_core.at[2 * D], sibling())
    deg_core.start()
    deg_core.wait()
    dacc[core] += dcore[...]

    def deg_xy(p):
        t = xy_to(p)
        return remote(dacc.at[core, t], dxy.at[p], s_xy.at[0], r_xy.at[D, 0], xy_dev(t))
    each(1, chips, lambda p: deg_xy(p).start())
    dz[0] = rowp[0, z, 0:8, 0:BS]
    dxy[0] = dacc[core, chip]
    remote(dz.at[1:], dz.at[1:], s_z.at[0], r_z.at[D, 0], z_dev(z_to(1))).wait()
    remote(dxy.at[1:], dxy.at[1:], s_xy.at[0], r_xy.at[D, 0], xy_dev(xy_to(1))).wait()
    degree = jnp.sum(dz[...], axis=0)[0:1] + jnp.sum(jnp.sum(dxy[...], axis=0), axis=0, keepdims=True)
    inv_row = 1.0 / jnp.sqrt(degree / BS + 1e-05)
    inv = jnp.broadcast_to(inv_row, (BS, BS)).T
    inv = inv[:, 0:1]
    yv[0] = start[...]

    def row_pos(k, t):
        return k * chips + t

    def apply_once(a, beside=lambda i: None):
        w = inv * yv[a]
        wc[(a % 2), pl.ds(pl.multiple_of(row_pos(core, chip) * BS, BS), BS), :] = w.astype(bf16)
        wt[a, :, pl.ds(pl.multiple_of(z * BS, BS), BS)] = w.T.astype(bf16)
        even = (a % 2)

        def wt_part(h, t):
            return wt.at[a, pl.ds(h * hw, hw), pl.ds(pl.multiple_of(t * BS, BS), BS)]

        def wc_part(h, k, t):
            return wc.at[even, pl.ds(pl.multiple_of(row_pos(k, t) * BS, BS), BS), pl.ds(h * hw, hw)]

        def z_send(h, p):
            return remote(wt_part(h, z), wt_part(h, z), s_z.at[h], r_z.at[a, h], z_dev(z_to(p)))

        def xy_send(h, p):
            part = wc_part(h, core, chip)
            return remote(part, part, s_xy.at[h], r_xy.at[a, h], xy_dev(xy_to(p)))

        def z_all(h):
            return remote(zsend.at[h, 1:], zrecv.at[a, h, 1:], s_z.at[h], r_z.at[a, h], z_dev(z_to(1)))

        def xy_all(h):
            return remote(rsend.at[h, 1:], rrecv.at[a, h, 1:], s_xy.at[h], r_xy.at[a, h], xy_dev(xy_to(1)))

        def rs_z_all(h):
            return remote(zsend.at[h, 1:], zrecv.at[a, h, 1:], s_rz.at[h], r_rz.at[a, h], z_dev(z_to(1)))

        def rs_xy_all(h):
            return remote(rsend.at[h, 1:], rrecv.at[a, h, 1:], s_rx.at[h], r_rx.at[a, h], xy_dev(xy_to(1)))

        def pass_on(h, k, g):
            first = row_pos(k, g * side) * BS
            part = wc.at[even, pl.ds(pl.multiple_of(first, BS), side * BS), pl.ds(h * hw, hw)]
            return remote(part, part, s_fwd.at[h, g], r_fwd.at[a, h * side + g], sibling())

        def swap(h):
            return remote(colq.at[h], corep.at[a, h], s_core.at[h], r_core.at[a * 2 + h], sibling())

        def rs_xy(h, p):
            return remote(rsend.at[h, p], rrecv.at[a, h, p], s_rx.at[h], r_rx.at[a, h], xy_dev(xy_to(p)))

        def rs_z(h, p):
            return remote(zsend.at[h, p], zrecv.at[a, h, p], s_rz.at[h], r_rz.at[a, h], z_dev(z_to(p)))

        def send_out(h):
            each(1, n_col, lambda p: z_send(h, p).start())
            each(1, chips, lambda p: xy_send(h, p).start())

        send_out(0)
        send_out(1)
        beside(0)

        def col_tiles(h, k, out_ref):
            def tile(n):
                first = (k * chips + 2 * n) * BS
                out = jnp.dot(wt[a, h * hw:(h + 1) * hw, :], u[:, pl.ds(pl.multiple_of(first, 2 * BS), 2 * BS)],
                              preferred_element_type=f32)
                out_ref[h, 2 * n] = out[:, :BS].astype(out_ref.dtype)
                out_ref[h, 2 * n + 1] = out[:, BS:].astype(out_ref.dtype)
            each(0, chips // 2, tile)

        for h in range(2):
            z_all(h).wait_recv()
            if h == 0:
                beside(1)
            col_tiles(h, other, colq)
            swap(h).start()
            col_tiles(h, core, colp)
            xy_all(h).wait_recv()
            each(0, side, lambda g: pass_on(h, core, g).start())
            if h == 0:
                beside(2)
            swap(h).wait_recv()

            def combine(p):
                t = xy_to(p)
                rsend[h, p] = (colp[h, t] + corep[a, h, t].astype(f32)).astype(bf16)
                rs_xy(h, p).start()
            each(1, chips, combine)
            each(0, side, lambda g: pass_on(h, other, g).wait_recv())

            def row_tile(n):
                out = jnp.dot(u[pl.ds(pl.multiple_of(n * 2 * BS, 2 * BS), 2 * BS), :],
                              wc[even, :, h * hw:(h + 1) * hw], preferred_element_type=f32)
                rowp[h, 2 * n] = out[:BS]
                rowp[h, 2 * n + 1] = out[BS:]
            each(0, n_col // 2, row_tile)

            def row_go(p):
                zsend[h, p] = rowp[h, z_to(p)].astype(bf16)
                rs_z(h, p).start()
            each(1, n_col, row_go)
            beside(3 + h)

        for h in range(2):
            rs_xy_all(h).wait_recv()
            cols = colp[h, chip] + corep[a, h, chip].astype(f32)
            for p in range(1, chips):
                cols = cols + rrecv[a, h, p].astype(f32)
            rs_z_all(h).wait_recv()
            rows = rowp[h, z]
            for p in range(1, n_col):
                rows = rows + zrecv[a, h, p].astype(f32)
            out = inv * (rows + cols.T)
            yv[a + 1, :, h * hw:(h + 1) * hw] = out
            ytv[a, h * hw:(h + 1) * hw, :] = out.T
        for h in range(2):
            swap(h).wait_send()
            for copies in (z_all(h), xy_all(h), rs_z_all(h), rs_xy_all(h)):
                copies.wait_send()
            each(0, side, lambda g: pass_on(h, core, g).wait_send())

    def local_gram(a, b, into, n):
        g = jnp.dot(ytv[a], yv[b], precision=highest, preferred_element_type=f32)
        g = g.reshape(2, chips, width // n_row, width)
        for k in range(2):
            for t in range(chips):
                into[k, t, n] = g[k, t]

    def sum_steps(bufs, base):
        gr, ga, gb, gc, gd = bufs
        q = 2 * base
        g_core = remote(gr.at[other], ga, t_core.at[0], q_core.at[q], sibling())
        g_last = remote(gd.at[core], gd.at[core], t_core.at[0], q_core.at[q + 1], sibling())

        def g_xy(p):
            t = xy_to(p)
            return remote(gr.at[core, t], gb.at[p], t_xy.at[q], q_xy.at[q], xy_dev(t))

        def g_z(p):
            return remote(gc.at[0], gc.at[p], t_z.at[base], q_z.at[base], z_dev(z_to(p)))

        def all_xy(k):
            return remote(ga.at[1:], gb.at[1:], t_xy.at[k], q_xy.at[k], xy_dev(xy_to(1)))

        def g_out(p):
            return remote(gd.at[core, chip], gd.at[core, chip], t_xy.at[q + 1], q_xy.at[q + 1], xy_dev(xy_to(p)))

        def add_z(t, total):
            return total + gc[lax.rem(z + n_col - t, n_col)]

        def step1():
            g_core.wait()
            gr[core] += ga[...]
            each(1, chips, lambda p: g_xy(p).start())

        def step2():
            all_xy(q).wait()
            gb[0] = gr[core, chip]
            gc[0] = jnp.sum(gb[...], axis=0)
            each(1, n_col, lambda p: g_z(p).start())

        def step3():
            remote(gc.at[1:], gc.at[1:], t_z.at[base], q_z.at[base], z_dev(z_to(1))).wait()
            gd[core, chip] = lax.fori_loop(1, n_col, add_z, gc[z])
            each(1, chips, lambda p: g_out(p).start())

        def step4():
            all_xy(q + 1).wait()
            g_last.start()

        def step5():
            g_last.wait_send()
            remote(gd.at[other], gd.at[other], t_core.at[0], q_core.at[q + 1], sibling()).wait_recv()

        return g_core.start, step1, step2, step3, step4, step5

    mul = functools.partial(jnp.dot, precision=highest, preferred_element_type=f32)
    tmul = lambda a, b: lax.dot_general(a, b, (((0,), (0,)), ((), ())), precision=highest, preferred_element_type=f32)
    s, e, li, half, full = chol

    gram_sum = sum_steps(gram_bufs, 0)

    def last_apply(i):
        if i == 0:
            local_gram(0, 1, gram_bufs[0], 0)
            local_gram(1, 2, gram_bufs[0], 1)
            gram_sum[0]()
            gram_sum[1]()
        else:
            gram_sum[i + 1]()
        if i == 4:
            first_factors()

    def first_factors():
        for m in range(2):
            full[m] = gram_bufs[4][:, :, m].reshape(width, width)
            s[m] = full[m, :BS, :BS]
        unit(e)
        panels(s, e, 0, BS // 8)
        for m in range(2):
            li[m, :BS, :BS] = e[m]
            li[m, :BS, BS:] = jnp.zeros((BS, BS), f32)
            half[m] = mul(e[m], full[m, :BS, BS:])
            s[m] = full[m, BS:, BS:] - tmul(half[m], half[m])
        unit(e)

    each(0, APPLIES - 1, apply_once, False)
    apply_once(APPLIES - 1, last_apply)
    local_gram(1, 3, ritz_bufs[0], 0)
    cuts = (0, 2, 7, 11, 16)

    def second_factors(i):
        if i < 4:
            panels(s, e, cuts[i], cuts[i + 1])
        else:
            for m in range(2):
                li[m, BS:, BS:] = e[m]
                li[m, BS:, :BS] = -mul(e[m], tmul(half[m], li[m, :BS, :BS]))
            gram = mul(mul(li[0], full[1]), li[0].T)
            scaled[...] = gram
            scales[1] = jnp.broadcast_to(
                1.0 / jnp.sqrt(jnp.sum(gram * gram, keepdims=True) / (width * width) + 1e-06), (8, BS))
            full[0] = li[1].T
            yv[0] = mul(yv[2], full[0])
            yv[1] = mul(yv[3], full[0])

    ritz_sum = sum_steps(ritz_bufs, 1)
    for i in range(5):
        ritz_sum[i]()
        second_factors(i)
    ritz_sum[5]()
    ritz = mul(mul(li[1], ritz_bufs[4][:, :, 0].reshape(width, width)), full[0])
    scales[0] = jnp.broadcast_to(1.0 / jnp.sqrt(jnp.sum(ritz * ritz, keepdims=True) / (width * width) + 1e-06), (8, BS))
    projected[...] = ritz
    basis[...] = yv[0]
    residual[...] = yv[1] - mul(yv[0], ritz)


def unit(e):
    eye = (lax.broadcasted_iota(jnp.int32, (BS, BS), 0) == lax.broadcasted_iota(jnp.int32, (BS, BS), 1)).astype(f32)
    for m in range(2):
        e[m] = eye


def fused(table, blocks, start, side, n_col, interpret=False):
    chips = side * side
    n_row = 2 * chips
    width = start.shape[1]
    sems = pltpu.SemaphoreType.DMA
    vmem = pltpu.VMEM
    part = width // n_row
    hw = width // 2
    tall = jax.ShapeDtypeStruct((BS, width), f32)
    square = jax.ShapeDtypeStruct((width, width), f32)

    def sum_bufs(n):
        return (vmem((2, chips, n, part, width), f32), vmem((chips, n, part, width), f32),
                vmem((chips, n, part, width), f32), vmem((n_col, n, part, width), f32),
                vmem((2, chips, n, part, width), f32))
    return pl.pallas_call(
        functools.partial(kernel, side, n_col, width),
        out_shape=(tall, square, tall, square, jax.ShapeDtypeStruct((2, 8, BS), f32)),
        in_specs=[pl.BlockSpec(memory_space=pltpu.SMEM), pl.BlockSpec(memory_space=pl.ANY), pl.BlockSpec(memory_space=pltpu.VMEM)],
        out_specs=tuple([pl.BlockSpec(memory_space=pltpu.VMEM)] * 5),
        scratch_shapes=[
            vmem((n_col * BS, n_row * BS), bf16),
            vmem((APPLIES, width, n_col * BS), bf16),
            vmem((2, n_row * BS, width), bf16),
            vmem((2, chips, hw, BS), f32),
            vmem((2, chips, hw, BS), bf16),
            vmem((APPLIES, 2, chips, hw, BS), bf16),
            vmem((2, chips, hw, BS), bf16),
            vmem((APPLIES, 2, chips, hw, BS), bf16),
            vmem((2, n_col, BS, hw), f32),
            vmem((2, n_col, BS, hw), bf16),
            vmem((APPLIES, 2, n_col, BS, hw), bf16),
            vmem((APPLIES + 1, BS, width), f32),
            vmem((APPLIES, width, BS), f32),
            vmem((2, chips, 8, BS), f32),
            vmem((chips, 8, BS), f32),
            vmem((chips, 8, BS), f32),
            vmem((n_col, 8, BS), f32),
            sum_bufs(2), sum_bufs(1),
            (vmem((2, BS, BS), f32), vmem((2, BS, BS), f32), vmem((2, width, width), f32),
             vmem((2, BS, BS), f32), vmem((2, width, width), f32)),
            sems((2,)), sems((2 * APPLIES + 1,)),
            sems((2,)), sems((APPLIES + 1, 2)),
            sems((2,)), sems((APPLIES + 1, 2)),
            sems((2, side)), sems((APPLIES, 2 * side)),
            sems((2,)), sems((APPLIES, 2)),
            sems((2,)), sems((APPLIES, 2)),
            sems((1,)), sems((4,)),
            sems((4,)), sems((4,)),
            sems((2,)), sems((2,)),
            vmem(blocks.shape, bf16), sems(()),
        ],
        compiler_params=pltpu.CompilerParams(
            collective_id=0, has_side_effects=True, vmem_limit_bytes=60 * 1024 * 1024),
        interpret=interpret,
    )(table, blocks, start)


def panels(s, e, lo, hi):
    sub = lax.broadcasted_iota(jnp.int32, (8, BS), 0)
    lane = lax.broadcasted_iota(jnp.int32, (8, BS), 1)

    def panel(k, c):
        first = pl.multiple_of(k * 8, 8)
        for m in range(2):
            r = s[m, pl.ds(first, 8), :]
            g = e[m, pl.ds(first, 8), :]
            own = jnp.where(lane >= first, jnp.where(lane < first + 8, r, 0.0), 0.0)
            cols = []
            for j in range(8):
                at_j = jnp.where(lane == first + j, own, 0.0)
                cols.append(jnp.broadcast_to(jnp.sum(at_j, axis=1, keepdims=True), (8, BS)))
            scale = jnp.zeros((8, BS), f32)
            for j in range(8):
                pivot = jnp.broadcast_to(cols[j][j:j + 1], (8, BS))
                mult = jnp.where(sub > j, cols[j] / pivot, 0.0)
                scale = jnp.where(sub == j, pivot, scale)
                r = r - mult * r[j:j + 1]
                g = g - mult * g[j:j + 1]
                for i in range(j + 1, 8):
                    cols[i] = cols[i] - mult * cols[i][j:j + 1]
            scale = 1.0 / jnp.sqrt(scale)
            v = r * scale
            g = g * scale
            e[m, pl.ds(first, 8), :] = g
            below = jnp.where(lane >= first + 8, v, 0.0)
            below = below.T
            trail, inverse = s[m], e[m]
            for j in range(8):
                trail = trail - below[:, j:j + 1] * v[j:j + 1]
                inverse = inverse - below[:, j:j + 1] * g[j:j + 1]
            s[m] = trail
            e[m] = inverse
        return c
    lax.fori_loop(lo, hi, panel, 0)


def local(block_values, block_index, block_count, start_vectors, interpret=False):
    n_row = lax.axis_size("row")
    n_col = lax.axis_size("col")
    side = math.isqrt(n_row // 2)
    chips = side * side
    blocks = block_values[0, 0]
    slots = blocks.shape[0]
    first, second = block_index[0, 0, 0], block_index[0, 0, 1]
    owner = second // n_col
    place = (first % n_col) * n_row + (owner % 2) * chips + owner // 2
    slot_ids = jnp.arange(slots, dtype=jnp.int32)
    place = jnp.where(slot_ids < block_count[0, 0], place, -1)
    spots = jnp.arange(n_row * n_col, dtype=jnp.int32)
    table = jnp.sum(jnp.where(place[None, :] == spots[:, None], slot_ids[None, :] + 1, 0), axis=1)

    parts = fused(table, blocks, start_vectors, side, n_col, interpret)
    total_rows = BS * n_row * n_col
    whole = pl.BlockSpec(memory_space=pltpu.VMEM)
    return pl.pallas_call(
        functools.partial(scale_kernel, math.sqrt(total_rows), math.sqrt(total_rows / start_vectors.shape[1])),
        out_shape=tuple(jax.ShapeDtypeStruct(p.shape, f32) for p in parts[:4]),
        in_specs=[whole] * 5,
        out_specs=(whole,) * 4,
        interpret=interpret,
    )(*parts)


def scale_kernel(tall, rest, subspace, ritz, residual, gram, scales, basis, projected, ritz_residual, gram_scaled):
    inverse_spread, inverse_size = scales[0, 0:1, 0:1], scales[1, 0:1, 0:1]
    basis[...] = subspace[...] * tall
    projected[...] = ritz[...] * inverse_spread
    ritz_residual[...] = residual[...] * (inverse_spread * rest)
    gram_scaled[...] = gram[...] * inverse_size


def solution(mesh):
    return jax.shard_map(
        local,
        mesh=mesh,
        in_specs=(
            P("row", "col", None, None, None),
            P("row", "col", None, None),
            P("row", "col"),
            P(("row", "col"), None),
        ),
        out_specs=(P(("row", "col"), None), P(), P(("row", "col"), None), P()),
        check_vma=False,
    )
```

```python
import functools
import math

import jax
import jax.numpy as jnp
from jax import lax
from jax.experimental import pallas as pl
from jax.experimental.pallas import tpu as pltpu
from jax.sharding import PartitionSpec as P

APPLIES = 3
MESH = pl.DeviceIdType.MESH
highest = lax.Precision.HIGHEST
f32 = jnp.float32
bf16 = jnp.bfloat16
BS = 128


def kernel(side, n_col, width, table, stored, start, basis, projected, residual, scaled, scales,
           u, wt, wc, colp, colq, corep, rsend, rrecv, rowp, zsend, zrecv, yv, ytv,
           dacc, dcore, dxy, dz, gram_bufs, ritz_bufs, chol,
           s_core, r_core, s_xy, r_xy, s_z, r_z, s_fwd, r_fwd, s_rx, r_rx, s_rz, r_rz,
           t_core, q_core, t_xy, q_xy, t_z, q_z, blocks, b_sem):
    chips = side * side
    n_row = 2 * chips
    hw = width // 2
    row = lax.axis_index("row")
    z = lax.axis_index("col")
    core = lax.rem(row, 2)
    chip = row // 2
    y, x = chip // side, lax.rem(chip, side)
    other = 1 - core

    def sibling():
        return (chip * 2 + other, z)

    def xy_to(p):
        return lax.rem(y + p // side, side) * side + lax.rem(x + lax.rem(p, side), side)

    def xy_from(p):
        return lax.rem(y + side - p // side, side) * side + lax.rem(x + side - lax.rem(p, side), side)

    def z_to(p):
        return lax.rem(z + p, n_col)

    def z_from(p):
        return lax.rem(z + n_col - p, n_col)

    def xy_dev(t):
        return (t * 2 + core, z)

    def z_dev(t):
        return (row, t)

    def remote(src, dst, send, recv, dev):
        return pltpu.make_async_remote_copy(
            src_ref=src, dst_ref=dst, send_sem=send, recv_sem=recv,
            device_id=dev, device_id_type=MESH)

    def each(lo, hi, body, unroll=True):
        def step(i, c):
            body(i)
            return c
        lax.fori_loop(lo, hi, step, 0, unroll=unroll)

    load = pltpu.make_async_copy(stored, blocks, b_sem)
    load.start()

    barrier = pltpu.get_barrier_semaphore()
    pl.semaphore_signal(barrier, inc=1, device_id=sibling(), device_id_type=MESH)
    each(1, chips, lambda p: pl.semaphore_signal(
        barrier, inc=1, device_id=xy_dev(xy_to(p)), device_id_type=MESH))
    each(1, n_col, lambda p: pl.semaphore_signal(
        barrier, inc=1, device_id=z_dev(z_to(p)), device_id_type=MESH))

    dacc[...] = jnp.zeros_like(dacc)
    ones = jnp.ones((8, BS), f32)

    def fill_row(lr):
        def fill(pos, total):
            slot = table[lr * n_row + pos]
            live = (slot > 0).astype(f32)
            block = blocks[jnp.maximum(slot - 1, 0)].astype(f32) * live
            u[pl.ds(pl.multiple_of(lr * BS, BS), BS), pl.ds(pl.multiple_of(pos * BS, BS), BS)] = block.astype(bf16)
            size = jnp.abs(block)
            dacc[pos // chips, lax.rem(pos, chips)] += jnp.sum(size.reshape(BS // 8, 8, BS), axis=0)
            return total + size
        total = lax.fori_loop(0, n_row, fill, jnp.zeros((BS, BS), f32), unroll=4)
        rowp[0, lr, 0:8, 0:BS] = lax.dot_general(
            ones, total, (((1,), (1,)), ((), ())), precision=highest, preferred_element_type=f32)
    load.wait()
    each(0, n_col, fill_row, False)

    pl.semaphore_wait(barrier, 1 + (chips - 1) + (n_col - 1))

    D = APPLIES

    def deg_z(p, lr, slot):
        return remote(rowp.at[0, lr, 0:8, 0:BS], dz.at[p], s_z.at[0], r_z.at[D, 0], z_dev(slot))
    each(1, n_col, lambda p: deg_z(p, z_to(p), z_to(p)).start())
    deg_core = remote(dacc.at[other], dcore, s_core.at[0], r_core.at[2 * D], sibling())
    deg_core.start()
    deg_core.wait()
    dacc[core] += dcore[...]

    def deg_xy(p):
        t = xy_to(p)
        return remote(dacc.at[core, t], dxy.at[p], s_xy.at[0], r_xy.at[D, 0], xy_dev(t))
    each(1, chips, lambda p: deg_xy(p).start())
    dz[0] = rowp[0, z, 0:8, 0:BS]
    dxy[0] = dacc[core, chip]
    remote(dz.at[1:], dz.at[1:], s_z.at[0], r_z.at[D, 0], z_dev(z_to(1))).wait()
    remote(dxy.at[1:], dxy.at[1:], s_xy.at[0], r_xy.at[D, 0], xy_dev(xy_to(1))).wait()
    degree = jnp.sum(dz[...], axis=0)[0:1] + jnp.sum(jnp.sum(dxy[...], axis=0), axis=0, keepdims=True)
    inv_row = 1.0 / jnp.sqrt(degree / BS + 1e-05)
    inv = jnp.broadcast_to(inv_row, (BS, BS)).T
    inv = inv[:, 0:1]
    yv[0] = start[...]

    def row_pos(k, t):
        return k * chips + t

    def apply_once(a, beside=lambda i: None):
        w = inv * yv[a]
        wc[(a % 2), pl.ds(pl.multiple_of(row_pos(core, chip) * BS, BS), BS), :] = w.astype(bf16)
        wt[a, :, pl.ds(pl.multiple_of(z * BS, BS), BS)] = w.T.astype(bf16)
        even = (a % 2)

        def wt_part(h, t):
            return wt.at[a, pl.ds(h * hw, hw), pl.ds(pl.multiple_of(t * BS, BS), BS)]

        def wc_part(h, k, t):
            return wc.at[even, pl.ds(pl.multiple_of(row_pos(k, t) * BS, BS), BS), pl.ds(h * hw, hw)]

        def z_send(h, p):
            return remote(wt_part(h, z), wt_part(h, z), s_z.at[h], r_z.at[a, h], z_dev(z_to(p)))

        def xy_send(h, p):
            part = wc_part(h, core, chip)
            return remote(part, part, s_xy.at[h], r_xy.at[a, h], xy_dev(xy_to(p)))

        def z_all(h):
            return remote(zsend.at[h, 1:], zrecv.at[a, h, 1:], s_z.at[h], r_z.at[a, h], z_dev(z_to(1)))

        def xy_all(h):
            return remote(rsend.at[h, 1:], rrecv.at[a, h, 1:], s_xy.at[h], r_xy.at[a, h], xy_dev(xy_to(1)))

        def rs_z_all(h):
            return remote(zsend.at[h, 1:], zrecv.at[a, h, 1:], s_rz.at[h], r_rz.at[a, h], z_dev(z_to(1)))

        def rs_xy_all(h):
            return remote(rsend.at[h, 1:], rrecv.at[a, h, 1:], s_rx.at[h], r_rx.at[a, h], xy_dev(xy_to(1)))

        def pass_on(h, k, g):
            first = row_pos(k, g * side) * BS
            part = wc.at[even, pl.ds(pl.multiple_of(first, BS), side * BS), pl.ds(h * hw, hw)]
            return remote(part, part, s_fwd.at[h, g], r_fwd.at[a, h * side + g], sibling())

        def swap(h):
            return remote(colq.at[h], corep.at[a, h], s_core.at[h], r_core.at[a * 2 + h], sibling())

        def rs_xy(h, p):
            return remote(rsend.at[h, p], rrecv.at[a, h, p], s_rx.at[h], r_rx.at[a, h], xy_dev(xy_to(p)))

        def rs_z(h, p):
            return remote(zsend.at[h, p], zrecv.at[a, h, p], s_rz.at[h], r_rz.at[a, h], z_dev(z_to(p)))

        def send_out(h):
            each(1, n_col, lambda p: z_send(h, p).start())
            each(1, chips, lambda p: xy_send(h, p).start())

        send_out(0)
        send_out(1)
        beside(0)

        def col_tiles(h, k, out_ref):
            def tile(n):
                first = (k * chips + 2 * n) * BS
                out = jnp.dot(wt[a, h * hw:(h + 1) * hw, :], u[:, pl.ds(pl.multiple_of(first, 2 * BS), 2 * BS)],
                              preferred_element_type=f32)
                out_ref[h, 2 * n] = out[:, :BS].astype(out_ref.dtype)
                out_ref[h, 2 * n + 1] = out[:, BS:].astype(out_ref.dtype)
            each(0, chips // 2, tile)

        for h in range(2):
            z_all(h).wait_recv()
            if h == 0:
                beside(1)
            col_tiles(h, other, colq)
            swap(h).start()
            col_tiles(h, core, colp)
            xy_all(h).wait_recv()
            each(0, side, lambda g: pass_on(h, core, g).start())
            if h == 0:
                beside(2)
            swap(h).wait_recv()

            def combine(p):
                t = xy_to(p)
                rsend[h, p] = (colp[h, t] + corep[a, h, t].astype(f32)).astype(bf16)
                rs_xy(h, p).start()
            each(1, chips, combine)
            each(0, side, lambda g: pass_on(h, other, g).wait_recv())

            def row_tile(n):
                out = jnp.dot(u[pl.ds(pl.multiple_of(n * 2 * BS, 2 * BS), 2 * BS), :],
                              wc[even, :, h * hw:(h + 1) * hw], preferred_element_type=f32)
                rowp[h, 2 * n] = out[:BS]
                rowp[h, 2 * n + 1] = out[BS:]
            each(0, n_col // 2, row_tile)

            def row_go(p):
                zsend[h, p] = rowp[h, z_to(p)].astype(bf16)
                rs_z(h, p).start()
            each(1, n_col, row_go)
            beside(3 + h)

        for h in range(2):
            rs_xy_all(h).wait_recv()
            cols = colp[h, chip] + corep[a, h, chip].astype(f32)
            for p in range(1, chips):
                cols = cols + rrecv[a, h, p].astype(f32)
            rs_z_all(h).wait_recv()
            rows = rowp[h, z]
            for p in range(1, n_col):
                rows = rows + zrecv[a, h, p].astype(f32)
            out = inv * (rows + cols.T)
            yv[a + 1, :, h * hw:(h + 1) * hw] = out
            ytv[a, h * hw:(h + 1) * hw, :] = out.T
        for h in range(2):
            swap(h).wait_send()
            for copies in (z_all(h), xy_all(h), rs_z_all(h), rs_xy_all(h)):
                copies.wait_send()
            each(0, side, lambda g: pass_on(h, core, g).wait_send())

    def local_gram(a, b, into, n):
        g = jnp.dot(ytv[a], yv[b], precision=highest, preferred_element_type=f32)
        g = g.reshape(2, chips, width // n_row, width)
        for k in range(2):
            for t in range(chips):
                into[k, t, n] = g[k, t]

    def sum_steps(bufs, base):
        gr, ga, gb, gc, gd = bufs
        q = 2 * base
        g_core = remote(gr.at[other], ga, t_core.at[0], q_core.at[q], sibling())
        g_last = remote(gd.at[core], gd.at[core], t_core.at[0], q_core.at[q + 1], sibling())

        def g_xy(p):
            t = xy_to(p)
            return remote(gr.at[core, t], gb.at[p], t_xy.at[q], q_xy.at[q], xy_dev(t))

        def g_z(p):
            return remote(gc.at[0], gc.at[p], t_z.at[base], q_z.at[base], z_dev(z_to(p)))

        def all_xy(k):
            return remote(ga.at[1:], gb.at[1:], t_xy.at[k], q_xy.at[k], xy_dev(xy_to(1)))

        def g_out(p):
            return remote(gd.at[core, chip], gd.at[core, chip], t_xy.at[q + 1], q_xy.at[q + 1], xy_dev(xy_to(p)))

        def add_z(t, total):
            return total + gc[lax.rem(z + n_col - t, n_col)]

        def step1():
            g_core.wait()
            gr[core] += ga[...]
            each(1, chips, lambda p: g_xy(p).start())

        def step2():
            all_xy(q).wait()
            gb[0] = gr[core, chip]
            gc[0] = jnp.sum(gb[...], axis=0)
            each(1, n_col, lambda p: g_z(p).start())

        def step3():
            remote(gc.at[1:], gc.at[1:], t_z.at[base], q_z.at[base], z_dev(z_to(1))).wait()
            gd[core, chip] = lax.fori_loop(1, n_col, add_z, gc[z])
            each(1, chips, lambda p: g_out(p).start())

        def step4():
            all_xy(q + 1).wait()
            g_last.start()

        def step5():
            g_last.wait_send()
            remote(gd.at[other], gd.at[other], t_core.at[0], q_core.at[q + 1], sibling()).wait_recv()

        return g_core.start, step1, step2, step3, step4, step5

    mul = functools.partial(jnp.dot, precision=highest, preferred_element_type=f32)
    tmul = lambda a, b: lax.dot_general(a, b, (((0,), (0,)), ((), ())), precision=highest, preferred_element_type=f32)
    s, e, li, half, full = chol

    gram_sum = sum_steps(gram_bufs, 0)

    def last_apply(i):
        if i == 0:
            local_gram(0, 1, gram_bufs[0], 0)
            local_gram(1, 2, gram_bufs[0], 1)
            gram_sum[0]()
            gram_sum[1]()
        else:
            gram_sum[i + 1]()
        if i == 4:
            first_factors()

    def first_factors():
        for m in range(2):
            full[m] = gram_bufs[4][:, :, m].reshape(width, width)
            s[m] = full[m, :BS, :BS]
        unit(e)
        panels(s, e, 0, BS // 8)
        for m in range(2):
            li[m, :BS, :BS] = e[m]
            li[m, :BS, BS:] = jnp.zeros((BS, BS), f32)
            half[m] = mul(e[m], full[m, :BS, BS:])
            s[m] = full[m, BS:, BS:] - tmul(half[m], half[m])
        unit(e)

    each(0, APPLIES - 1, apply_once, False)
    apply_once(APPLIES - 1, last_apply)
    local_gram(1, 3, ritz_bufs[0], 0)
    cuts = (0, 2, 7, 11, 16)

    def second_factors(i):
        if i < 4:
            panels(s, e, cuts[i], cuts[i + 1])
        else:
            for m in range(2):
                li[m, BS:, BS:] = e[m]
                li[m, BS:, :BS] = -mul(e[m], tmul(half[m], li[m, :BS, :BS]))
            gram = mul(mul(li[0], full[1]), li[0].T)
            scaled[...] = gram
            scales[1] = jnp.broadcast_to(
                1.0 / jnp.sqrt(jnp.sum(gram * gram, keepdims=True) / (width * width) + 1e-06), (8, BS))
            full[0] = li[1].T
            yv[0] = mul(yv[2], full[0])
            yv[1] = mul(yv[3], full[0])

    ritz_sum = sum_steps(ritz_bufs, 1)
    for i in range(5):
        ritz_sum[i]()
        second_factors(i)
    ritz_sum[5]()
    ritz = mul(mul(li[1], ritz_bufs[4][:, :, 0].reshape(width, width)), full[0])
    scales[0] = jnp.broadcast_to(1.0 / jnp.sqrt(jnp.sum(ritz * ritz, keepdims=True) / (width * width) + 1e-06), (8, BS))
    projected[...] = ritz
    basis[...] = yv[0]
    residual[...] = yv[1] - mul(yv[0], ritz)


def unit(e):
    eye = (lax.broadcasted_iota(jnp.int32, (BS, BS), 0) == lax.broadcasted_iota(jnp.int32, (BS, BS), 1)).astype(f32)
    for m in range(2):
        e[m] = eye


def fused(table, blocks, start, side, n_col, interpret=False):
    chips = side * side
    n_row = 2 * chips
    width = start.shape[1]
    sems = pltpu.SemaphoreType.DMA
    vmem = pltpu.VMEM
    part = width // n_row
    hw = width // 2
    tall = jax.ShapeDtypeStruct((BS, width), f32)
    square = jax.ShapeDtypeStruct((width, width), f32)

    def sum_bufs(n):
        return (vmem((2, chips, n, part, width), f32), vmem((chips, n, part, width), f32),
                vmem((chips, n, part, width), f32), vmem((n_col, n, part, width), f32),
                vmem((2, chips, n, part, width), f32))
    return pl.pallas_call(
        functools.partial(kernel, side, n_col, width),
        out_shape=(tall, square, tall, square, jax.ShapeDtypeStruct((2, 8, BS), f32)),
        in_specs=[pl.BlockSpec(memory_space=pltpu.SMEM), pl.BlockSpec(memory_space=pl.ANY), pl.BlockSpec(memory_space=pltpu.VMEM)],
        out_specs=tuple([pl.BlockSpec(memory_space=pltpu.VMEM)] * 5),
        scratch_shapes=[
            vmem((n_col * BS, n_row * BS), bf16),
            vmem((APPLIES, width, n_col * BS), bf16),
            vmem((2, n_row * BS, width), bf16),
            vmem((2, chips, hw, BS), f32),
            vmem((2, chips, hw, BS), bf16),
            vmem((APPLIES, 2, chips, hw, BS), bf16),
            vmem((2, chips, hw, BS), bf16),
            vmem((APPLIES, 2, chips, hw, BS), bf16),
            vmem((2, n_col, BS, hw), f32),
            vmem((2, n_col, BS, hw), bf16),
            vmem((APPLIES, 2, n_col, BS, hw), bf16),
            vmem((APPLIES + 1, BS, width), f32),
            vmem((APPLIES, width, BS), f32),
            vmem((2, chips, 8, BS), f32),
            vmem((chips, 8, BS), f32),
            vmem((chips, 8, BS), f32),
            vmem((n_col, 8, BS), f32),
            sum_bufs(2), sum_bufs(1),
            (vmem((2, BS, BS), f32), vmem((2, BS, BS), f32), vmem((2, width, width), f32),
             vmem((2, BS, BS), f32), vmem((2, width, width), f32)),
            sems((2,)), sems((2 * APPLIES + 1,)),
            sems((2,)), sems((APPLIES + 1, 2)),
            sems((2,)), sems((APPLIES + 1, 2)),
            sems((2, side)), sems((APPLIES, 2 * side)),
            sems((2,)), sems((APPLIES, 2)),
            sems((2,)), sems((APPLIES, 2)),
            sems((1,)), sems((4,)),
            sems((4,)), sems((4,)),
            sems((2,)), sems((2,)),
            vmem(blocks.shape, bf16), sems(()),
        ],
        compiler_params=pltpu.CompilerParams(
            collective_id=0, has_side_effects=True, vmem_limit_bytes=60 * 1024 * 1024),
        interpret=interpret,
    )(table, blocks, start)


def panels(s, e, lo, hi):
    sub = lax.broadcasted_iota(jnp.int32, (8, BS), 0)
    lane = lax.broadcasted_iota(jnp.int32, (8, BS), 1)

    def panel(k, c):
        first = pl.multiple_of(k * 8, 8)
        for m in range(2):
            r = s[m, pl.ds(first, 8), :]
            g = e[m, pl.ds(first, 8), :]
            own = jnp.where(lane >= first, jnp.where(lane < first + 8, r, 0.0), 0.0)
            cols = []
            for j in range(8):
                at_j = jnp.where(lane == first + j, own, 0.0)
                cols.append(jnp.broadcast_to(jnp.sum(at_j, axis=1, keepdims=True), (8, BS)))
            scale = jnp.zeros((8, BS), f32)
            for j in range(8):
                pivot = jnp.broadcast_to(cols[j][j:j + 1], (8, BS))
                mult = jnp.where(sub > j, cols[j] / pivot, 0.0)
                scale = jnp.where(sub == j, pivot, scale)
                r = r - mult * r[j:j + 1]
                g = g - mult * g[j:j + 1]
                for i in range(j + 1, 8):
                    cols[i] = cols[i] - mult * cols[i][j:j + 1]
            scale = 1.0 / jnp.sqrt(scale)
            v = r * scale
            g = g * scale
            e[m, pl.ds(first, 8), :] = g
            below = jnp.where(lane >= first + 8, v, 0.0)
            below = below.T
            trail, inverse = s[m], e[m]
            for j in range(8):
                trail = trail - below[:, j:j + 1] * v[j:j + 1]
                inverse = inverse - below[:, j:j + 1] * g[j:j + 1]
            s[m] = trail
            e[m] = inverse
        return c
    lax.fori_loop(lo, hi, panel, 0)


def local(block_values, block_index, block_count, start_vectors, interpret=False):
    n_row = lax.axis_size("row")
    n_col = lax.axis_size("col")
    side = math.isqrt(n_row // 2)
    chips = side * side
    blocks = block_values[0, 0]
    slots = blocks.shape[0]
    first, second = block_index[0, 0, 0], block_index[0, 0, 1]
    owner = second // n_col
    place = (first % n_col) * n_row + (owner % 2) * chips + owner // 2
    slot_ids = jnp.arange(slots, dtype=jnp.int32)
    place = jnp.where(slot_ids < block_count[0, 0], place, -1)
    spots = jnp.arange(n_row * n_col, dtype=jnp.int32)
    table = jnp.sum(jnp.where(place[None, :] == spots[:, None], slot_ids[None, :] + 1, 0), axis=1)

    parts = fused(table, blocks, start_vectors, side, n_col, interpret)
    total_rows = BS * n_row * n_col
    whole = pl.BlockSpec(memory_space=pltpu.VMEM)
    return pl.pallas_call(
        functools.partial(scale_kernel, math.sqrt(total_rows), math.sqrt(total_rows / start_vectors.shape[1])),
        out_shape=tuple(jax.ShapeDtypeStruct(p.shape, f32) for p in parts[:4]),
        in_specs=[whole] * 5,
        out_specs=(whole,) * 4,
        interpret=interpret,
    )(*parts)


def scale_kernel(tall, rest, subspace, ritz, residual, gram, scales, basis, projected, ritz_residual, gram_scaled):
    inverse_spread, inverse_size = scales[0, 0:1, 0:1], scales[1, 0:1, 0:1]
    basis[...] = subspace[...] * tall
    projected[...] = ritz[...] * inverse_spread
    ritz_residual[...] = residual[...] * (inverse_spread * rest)
    gram_scaled[...] = gram[...] * inverse_size


def solution(mesh):
    return jax.shard_map(
        local,
        mesh=mesh,
        in_specs=(
            P("row", "col", None, None, None),
            P("row", "col", None, None),
            P("row", "col"),
            P(("row", "col"), None),
        ),
        out_specs=(P(("row", "col"), None), P(), P(("row", "col"), None), P()),
        check_vma=False,
    )
```
